128 devices in a mesh: dp: 8 (over x, core), fsdp: 16 (over y, z).
Axes of the slice: x: 4, y: 4, z: 4, core: 2. Of those that a mesh axis runs over, the one named last changes fastest.
Arguments:
- block_input: float32 [16384, 1024], P(('dp', 'fsdp')), may hold values from -6 to 6
- counts: int32 [8, 16], replicated, may hold values from 1 to 128, as said below
- query_weight: float32 [1, 1024, 2048], P(None, ('dp', 'fsdp')), may hold values from -0.1875 to 0.1875
- key_matrix: float32 [1, 1024, 1024], P(None, ('dp', 'fsdp')), may hold values from -0.1875 to 0.1875
- value_matrix: float32 [1, 1024, 1024], P(None, ('dp', 'fsdp')), may hold values from -0.1875 to 0.1875
- out_weight: float32 [1, 2048, 1024], P(None, ('dp', 'fsdp')), may hold values from -2 to 2
- gate_weight: float32 [1, 1024, 3072], P(None, ('dp', 'fsdp')), may hold values from -0.1875 to 0.1875
- up_weight: float32 [1, 1024, 3072], P(None, ('dp', 'fsdp')), may hold values from -0.1875 to 0.1875
- down_weight: float32 [1, 3072, 1024], P(None, ('dp', 'fsdp')), may hold values from -0.109375 to 0.109375
- attn_gain: float32 [1, 1024], P(None, ('dp', 'fsdp')), may hold values from 0.25 to 1.75
- mlp_gain: float32 [1, 1024], P(None, ('dp', 'fsdp')), may hold values from 0.25 to 1.75
- query_gain: float32 [1, 128], P(None, ('dp', 'fsdp')), may hold values from 0.25 to 1.75
- key_gain: float32 [1, 128], P(None, ('dp', 'fsdp')), may hold values from 0.25 to 1.75
- cotangent: float32 [16384, 1024], P(('dp', 'fsdp')), may hold values from -6 to 6
Outputs:
- block_output: float32 [16384, 1024], P(('dp', 'fsdp'))
- input_grad: float32 [16384, 1024], P(('dp', 'fsdp'))
- query_weight_grad: float32 [1, 1024, 2048], P(None, ('dp', 'fsdp'))
- key_weight_grad: float32 [1, 1024, 1024], P(None, ('dp', 'fsdp'))
- value_weight_grad: float32 [1, 1024, 1024], P(None, ('dp', 'fsdp'))
- out_weight_grad: float32 [1, 2048, 1024], P(None, ('dp', 'fsdp'))
- gate_weight_grad: float32 [1, 1024, 3072], P(None, ('dp', 'fsdp'))
- up_weight_grad: float32 [1, 1024, 3072], P(None, ('dp', 'fsdp'))
- down_weight_grad: float32 [1, 3072, 1024], P(None, ('dp', 'fsdp'))
- attn_gain_grad: float32 [1, 1024], P(None, ('dp', 'fsdp'))
- mlp_gain_grad: float32 [1, 1024], P(None, ('dp', 'fsdp'))
- query_gain_grad: float32 [1, 128], P(None, ('dp', 'fsdp'))
- key_gain_gradient: float32 [1, 128], P(None, ('dp', 'fsdp'))
The draws below stay inside these ranges and needn't reach their ends.
Inputs may be any that keep to these rules, and one draw needn't show every extreme that they name: counts[g, d] slots of device d of group g are filled, from its first slot on; the rest are padding. The filled slots of a group, in device order, form one sequence. Device 0 of every group is full.
All inputs are finite; a program needn't handle non-finite values.
Results may differ from the reference program's by a relative error of at most 0.03.
Values may be sent and summed in bfloat16 or wider, within the bound.
No kernel may reach another device: no remote copies, remote signals or barrier semaphores. Data moves between devices by JAX's collectives and lax.ppermute only.
A program may use at most 192 MiB of HBM per device.

```python
import jax
import jax.numpy as jnp
from jax import lax

MODEL_WIDTH = 1024
QUERY_HEADS = 16
KEY_VALUE_HEADS = 8
HEAD_SIZE = 128
FF = 3072
DECODER_LAYERS = 1
SEQUENCE_SLOTS = 2048
TOK_ROWS = 128
TOTAL_TOKENS = 16384
N_DP = 8
N_FSDP = 16


def draw_counts(key, part):
    key = jax.random.fold_in(key, 11)
    floor_key, fill_key = jax.random.split(key)
    floors = jax.random.randint(floor_key, (N_DP, 1), 1, TOK_ROWS + 1)
    raw_fill = jax.random.randint(fill_key, (N_DP, N_FSDP), 0, TOK_ROWS)
    filled = floors + raw_fill * (TOK_ROWS + 1 - floors) // TOK_ROWS
    first_column = jnp.arange(N_FSDP)[None, :] == 0
    return jnp.where(first_column, TOK_ROWS, filled).astype(jnp.int32)


def block_levels(stream_key, dims, cuts, least, largest):
    def one(dim, blocks):
        heights = jax.random.uniform(jax.random.fold_in(jax.random.fold_in(stream_key, 6), dim), (blocks,), jnp.float32, least / len(cuts), largest / len(cuts))
        return jnp.repeat(jnp.exp(heights), dims[dim] // blocks).reshape((-1,) + (1,) * (len(dims) - dim - 1))

    factor_of = one(*cuts[0])
    for cut in cuts[1:]:
        factor_of = factor_of * one(*cut)
    return factor_of


def scatter_about(stream_key, shape, spread, reach, pieces=(), kind=jnp.bfloat16):
    gain = block_levels(stream_key, shape, pieces, -0.22, 0.18) if pieces else 1.0
    result = jax.random.normal(stream_key, shape, jnp.float32) * spread * gain
    return jnp.minimum(jnp.maximum(result, -reach), reach).astype(kind)


def setup_inputs(seed: int = 0) -> dict:
    key_list = jax.random.split(jax.random.key(seed), 15)
    block_input = scatter_about(key_list[0], (TOTAL_TOKENS, MODEL_WIDTH), 1.0, 6.0, ((0, 128),), jnp.float32)
    counts = draw_counts(jax.random.fold_in(key_list[14], 71), 0)
    query_weight = scatter_about(key_list[2], (DECODER_LAYERS, MODEL_WIDTH, QUERY_HEADS * HEAD_SIZE), MODEL_WIDTH ** -0.5, 0.1875, ((1, 128),), jnp.float32)
    key_matrix = scatter_about(key_list[3], (DECODER_LAYERS, MODEL_WIDTH, KEY_VALUE_HEADS * HEAD_SIZE), MODEL_WIDTH ** -0.5, 0.1875, ((1, 128),), jnp.float32)
    value_matrix = scatter_about(key_list[4], (DECODER_LAYERS, MODEL_WIDTH, KEY_VALUE_HEADS * HEAD_SIZE), MODEL_WIDTH ** -0.5, 0.1875, ((1, 128),), jnp.float32)
    out_weight = scatter_about(key_list[5], (DECODER_LAYERS, QUERY_HEADS * HEAD_SIZE, MODEL_WIDTH), (QUERY_HEADS * HEAD_SIZE // 256) ** -0.5, 2.0, ((1, 128),), jnp.float32)
    gate_weight = scatter_about(key_list[6], (DECODER_LAYERS, MODEL_WIDTH, FF), MODEL_WIDTH ** -0.5, 0.1875, ((1, 128),), jnp.float32)
    up_weight = scatter_about(key_list[7], (DECODER_LAYERS, MODEL_WIDTH, FF), MODEL_WIDTH ** -0.5, 0.1875, ((1, 128),), jnp.float32)
    down_weight = scatter_about(key_list[8], (DECODER_LAYERS, FF, MODEL_WIDTH), FF ** -0.5, 0.109375, ((1, 128),), jnp.float32)
    attn_gain = jnp.clip(1.0 + 0.15 * jax.random.normal(key_list[9], (DECODER_LAYERS, MODEL_WIDTH), jnp.float32), 0.25, 1.75)
    mlp_gain = jnp.clip(1.0 + 0.15 * jax.random.normal(key_list[10], (DECODER_LAYERS, MODEL_WIDTH), jnp.float32), 0.25, 1.75)
    query_gain = jnp.clip(1.0 + 0.15 * jax.random.normal(key_list[11], (DECODER_LAYERS, HEAD_SIZE), jnp.float32), 0.25, 1.75)
    key_gain = jnp.clip(1.0 + 0.15 * jax.random.normal(key_list[12], (DECODER_LAYERS, HEAD_SIZE), jnp.float32), 0.25, 1.75)
    cotangent = scatter_about(key_list[13], (TOTAL_TOKENS, MODEL_WIDTH), 1.0, 6.0, ((0, 128),), jnp.float32)
    return dict(block_input=block_input, counts=counts, query_weight=query_weight, key_matrix=key_matrix, value_matrix=value_matrix, out_weight=out_weight, gate_weight=gate_weight, up_weight=up_weight, down_weight=down_weight, attn_gain=attn_gain, mlp_gain=mlp_gain, query_gain=query_gain, key_gain=key_gain, cotangent=cotangent)


EPSILON = 1e-06
ROPE_BASE = 1000000.0
BLOCKED_SCORE = -1e+30
HIGHEST = lax.Precision.HIGHEST

@jax.custom_vjp
def low(v):
    return lax.optimization_barrier(v.astype(jnp.bfloat16)).astype(jnp.float32)

@jax.custom_vjp
def low_back(v):
    return v

def low_keep(v):
    return (low(v), None)

def low_pass(kept, grad):
    return (grad,)

def back_keep(v):
    return (v, None)

def back_low(kept, grad):
    return (low(grad),)
low.defvjp(low_keep, low_pass)
low_back.defvjp(back_keep, back_low)

def norm_apply(values, gain_vec):
    return values * lax.rsqrt(lax.optimization_barrier(jnp.mean(values * values, -1, keepdims=True)) + EPSILON) * gain_vec

def rotate(values, token_positions):
    half_width = values.shape[-1] // 2
    inverse = ROPE_BASE ** (-(jnp.arange(half_width, dtype=jnp.float32) * 2.0 / values.shape[-1]))
    angles = token_positions.astype(jnp.float32)[:, None] * inverse[None, :]
    cosine = jnp.cos(angles)[:, None, :]
    sine_part = jnp.sin(angles)[:, None, :]
    first_half = values[..., :half_width]
    second_half = values[..., half_width:]
    return jnp.concatenate([first_half * cosine - second_half * sine_part, second_half * cosine + first_half * sine_part], -1)

def head_apply(projected, gain_vec, token_positions):
    shaped = projected.reshape(projected.shape[0], -1, gain_vec.shape[0])
    return rotate(norm_apply(shaped, gain_vec), token_positions)

def positions_of(counts):
    offsets = jnp.arange(TOK_ROWS, dtype=jnp.int32)
    starts = jnp.cumsum(counts, axis=1) - counts
    token_positions = (starts[:, :, None] + offsets[None, None, :]).reshape(TOTAL_TOKENS).astype(jnp.int32)
    active_mask = (offsets[None, None, :] < counts[:, :, None]).reshape(TOTAL_TOKENS)
    return (token_positions, active_mask)

def attend_rows(query_block, query_pos, key_row_matrix, value_row_matrix, key_pos, key_live):
    raw_scores = jnp.einsum('rhgd,khd->hgrk', query_block, key_row_matrix, precision=HIGHEST)
    scores = low_back(raw_scores) * HEAD_SIZE ** (-0.5)
    allowed = (key_pos[None, :] <= query_pos[:, None]) & key_live[None, :]
    scores = jnp.where(allowed, scores, BLOCKED_SCORE)
    top_score = lax.optimization_barrier(jnp.max(scores, -1, keepdims=True))
    log_total = top_score + jnp.log(lax.optimization_barrier(jnp.sum(jnp.exp(scores - top_score), -1, keepdims=True)))
    weights = low(jnp.exp(scores - log_total))
    mixed_heads = jnp.einsum('hgrk,khd->rhgd', weights, value_row_matrix, precision=HIGHEST)
    return low(low_back(mixed_heads))

def attend_group(packed_tokens):
    query_rows, key_row_matrix, value_row_matrix, token_positions, active_mask = packed_tokens
    block_length = min(512, SEQUENCE_SLOTS)
    count_of_blocks = SEQUENCE_SLOTS // block_length

    def one_block(block_item):
        query_block, query_pos = block_item
        return attend_rows(query_block, query_pos, key_row_matrix, value_row_matrix, token_positions, active_mask)
    query_block_list = query_rows.reshape(count_of_blocks, block_length, KEY_VALUE_HEADS, QUERY_HEADS // KEY_VALUE_HEADS, HEAD_SIZE)
    pos_blocks = token_positions.reshape(count_of_blocks, block_length)
    mixed_heads = lax.map(jax.checkpoint(one_block), (query_block_list, pos_blocks))
    return mixed_heads.reshape(SEQUENCE_SLOTS, QUERY_HEADS * HEAD_SIZE)

def attention_layer(query_rows, key_row_matrix, value_row_matrix, token_positions, active_mask):
    packed_tokens = (query_rows.reshape(N_DP, SEQUENCE_SLOTS, KEY_VALUE_HEADS, QUERY_HEADS // KEY_VALUE_HEADS, HEAD_SIZE), key_row_matrix.reshape(N_DP, SEQUENCE_SLOTS, KEY_VALUE_HEADS, HEAD_SIZE), value_row_matrix.reshape(N_DP, SEQUENCE_SLOTS, KEY_VALUE_HEADS, HEAD_SIZE), token_positions.reshape(N_DP, SEQUENCE_SLOTS), active_mask.reshape(N_DP, SEQUENCE_SLOTS))
    return lax.map(jax.checkpoint(attend_group), packed_tokens).reshape(TOTAL_TOKENS, QUERY_HEADS * HEAD_SIZE)

def layer_forward(hidden, weights, token_positions, active_mask):
    query_weight, key_matrix, value_matrix, out_weight, gate_weight, up_weight, down_weight, attn_gain, mlp_gain, query_gain, key_gain = weights
    normed = low(norm_apply(hidden, low(attn_gain)))
    query_proj = low_back(jnp.dot(normed, low(query_weight), precision=HIGHEST))
    key_proj = low_back(jnp.dot(normed, low(key_matrix), precision=HIGHEST))
    value_projection = low(low_back(jnp.dot(normed, low(value_matrix), precision=HIGHEST)))
    query_rows = low(head_apply(query_proj, low(query_gain), token_positions))
    key_row_matrix = low(head_apply(key_proj, low(key_gain), token_positions))
    mixed_flattened = attention_layer(query_rows, key_row_matrix, value_projection.reshape(TOTAL_TOKENS, KEY_VALUE_HEADS, HEAD_SIZE), token_positions, active_mask)
    middle = hidden + low_back(jnp.dot(mixed_flattened, low(out_weight), precision=HIGHEST))
    second_normed = low(norm_apply(middle, low(mlp_gain)))
    gate_proj = low_back(jnp.dot(second_normed, low(gate_weight), precision=HIGHEST))
    up_proj = low_back(jnp.dot(second_normed, low(up_weight), precision=HIGHEST))
    inner_act = low(gate_proj * jax.nn.sigmoid(gate_proj) * up_proj)
    return middle + low_back(jnp.dot(inner_act, low(down_weight), precision=HIGHEST))

def reference(block_input, counts, query_weight, key_matrix, value_matrix, out_weight, gate_weight, up_weight, down_weight, attn_gain, mlp_gain, query_gain, key_gain, cotangent):
    token_positions, active_mask = positions_of(counts)

    def forward(hidden, query_all, key_all, value_all, out_all, gate_all, up_all, down_all, attn_all, mlp_all, qgain_all, kgain_all):
        for layer_index in range(DECODER_LAYERS):
            weights = (query_all[layer_index], key_all[layer_index], value_all[layer_index], out_all[layer_index], gate_all[layer_index], up_all[layer_index], down_all[layer_index], attn_all[layer_index], mlp_all[layer_index], qgain_all[layer_index], kgain_all[layer_index])
            hidden = layer_forward(hidden, weights, token_positions, active_mask)
        return hidden
    block_output, pullback = jax.vjp(forward, block_input, query_weight, key_matrix, value_matrix, out_weight, gate_weight, up_weight, down_weight, attn_gain, mlp_gain, query_gain, key_gain)
    gradients = pullback(cotangent * active_mask[:, None].astype(jnp.float32))
    return (block_output, gradients[0], gradients[1], gradients[2], gradients[3], gradients[4], gradients[5], gradients[6], gradients[7], gradients[8], gradients[9], gradients[10], gradients[11])
```

```python
import functools

import jax
import jax.numpy as jnp
from jax import lax
from jax.experimental import pallas as pl
from jax.experimental.pallas import tpu as pltpu
from jax.sharding import Mesh, PartitionSpec as P

HEADS = 16
KV_HEADS = 8
SIZE = 128
WIDTH = 1024
ROWS = 128
PLACES = 16
EPSILON = 1e-06
ROPE_BASE = 1000000.0
SCALE = SIZE**-0.5
SCALE2 = SCALE * 1.4426950408889634
F32 = jnp.float32
BF16 = jnp.bfloat16
MIB = 1 << 20

TOKENS = ("y", "z")
ALL = ("x", "core", "y", "z")

UNITS = 11
HALVES = [(u, c) for u in range(UNITS) for c in range(2)]
PARTS = [HALVES[:11], HALVES[11:]]
ORDERS = (("x", "y"), ("y", "x"))
MASKS = ((1, 3), (3, 1))
KEPT = ((0, 3, 1, 2), (0, 1, 3, 2))
QUARTERS = [(p, m, h) for p in range(2) for m, h in enumerate((PARTS[p][:6], PARTS[p][6:]))]
PAIRS = [(0, 0), (1, 0)] + [(2, 1 + t) for t in range(6)] + [(3 + t, 7) for t in range(3)]


def matmul(a, b):
    return lax.dot_general(a, b, (((1,), (0,)), ((), ())), preferred_element_type=F32)


def matmul_nt(a, b):
    return lax.dot_general(a, b, (((1,), (1,)), ((), ())), preferred_element_type=F32)


def matmul_tn(a, b):
    return lax.dot_general(a, b, (((0,), (0,)), ((), ())), preferred_element_type=F32)


def exact(a, b):
    return lax.dot_general(
        a, b, (((1,), (0,)), ((), ())), preferred_element_type=F32, precision=lax.Precision.HIGHEST
    )


SMEM = pl.BlockSpec(memory_space=pltpu.SMEM)
HBM = pl.BlockSpec(memory_space=pltpu.HBM)


class Moves:
    def __init__(self, ins, outs, sems):
        self.ins, self.outs, self.sems, self.sent, self.pushed = ins, outs, sems, [], 0

    def need(self, *which):
        for i in which or list(self.ins):
            if i in self.ins:
                self.ins.pop(i).wait()

    def flush(self, *which):
        for i in which or list(self.outs):
            if i in self.outs:
                copy = self.outs.pop(i)
                copy.start()
                self.sent.append(copy)

    def push(self, source, target):
        copy = pltpu.make_async_copy(source, target, self.sems.at[self.pushed])
        copy.start()
        self.sent.append(copy)
        self.pushed += 1

    def finish(self):
        self.need()
        self.flush()
        for copy in self.sent:
            copy.wait()


def call(
    kernel, outs, args, scalars=(), anywhere=(), raw=(), scratch=(), limit=60, flops=0, nbytes=0, sends=0
):
    moved = [i for i in range(len(args)) if i not in scalars and i not in anywhere]
    made = [i for i in range(len(outs)) if i not in raw]
    count, total = len(args), len(outs)

    def body(*refs):
        ins, out, rest = list(refs[:count]), list(refs[count : count + total]), list(refs[count + total :])
        here = [rest.pop(0) for i in moved]
        there = [rest.pop(0) for i in made]
        sems_in, sems_out = rest.pop(0), rest.pop(0)
        copies_in = {i: pltpu.make_async_copy(ins[i], here[n], sems_in.at[n]) for n, i in enumerate(moved)}
        copies_out = {
            i: pltpu.make_async_copy(there[n], out[i], sems_out.at[sends + n]) for n, i in enumerate(made)
        }
        for copy in copies_in.values():
            copy.start()
        for n, i in enumerate(moved):
            ins[i] = here[n]
        for n, i in enumerate(made):
            out[i] = there[n]
        moves = Moves(copies_in, copies_out, sems_out)
        kernel(moves, *ins, *out, *rest)
        moves.finish()

    buffers = [pltpu.VMEM(args[i].shape, args[i].dtype) for i in moved]
    buffers += [pltpu.VMEM(*outs[i]) for i in made]
    sems = [pltpu.SemaphoreType.DMA((max(len(moved), 1),)), pltpu.SemaphoreType.DMA((len(made) + sends,))]
    return pl.pallas_call(
        body,
        out_shape=[jax.ShapeDtypeStruct(s, t) for s, t in outs],
        in_specs=[SMEM if i in scalars else HBM for i in range(count)],
        out_specs=[HBM] * total,
        scratch_shapes=buffers + sems + list(scratch),
        compiler_params=pltpu.CompilerParams(vmem_limit_bytes=limit * MIB),
        cost_estimate=pl.CostEstimate(flops=flops, bytes_accessed=nbytes, transcendentals=0),
    )(*args)


def iota(shape, dim):
    return lax.broadcasted_iota(jnp.int32, shape, dim)


def mean_scale(v):
    return lax.rsqrt(jnp.mean(v * v, -1, keepdims=True) + EPSILON)


def norm_back(grad, normal, scale):
    return scale * (grad - normal * jnp.mean(grad * normal, -1, keepdims=True))


def swap_halves(v):
    return pltpu.roll(v, 64, 1)


def column(row):
    return jnp.sum(jnp.where(iota((8, 8), 0) == iota((8, 8), 1), row, 0.0), 1, keepdims=True)


def hidden_map(back):
    shape = (384, 384)
    source, target = (iota(shape, 1), iota(shape, 0)) if back else (iota(shape, 0), iota(shape, 1))
    i, rest = source // 24, source % 24
    return jnp.where((rest // 8) * 128 + i * 8 + rest % 8 == target, 1.0, 0.0)


def channel_map(back):
    shape = (128, 128)
    source, target = (iota(shape, 1), iota(shape, 0)) if back else (iota(shape, 0), iota(shape, 1))
    i, rest = source // 16, source % 16
    return jnp.where((rest // 8) * 64 + i * 8 + rest % 8 == target, 1.0, 0.0)


def prepare_kernel(moves, x_ref, o_ref, g_ref, u_ref, d_ref, g2_ref, ff_ref, n0_ref, n1_ref):
    moves.need(0)
    x = x_ref[...]
    normal = (x * mean_scale(x)).astype(BF16)
    n0_ref[...] = normal[:, :512]
    n1_ref[...] = normal[:, 512:]
    moves.flush(1, 2)
    moves.need()
    gain2 = column(g2_ref[...].astype(BF16).astype(F32))
    for t in range(2):
        ff_ref[t] = o_ref[0, 8 * t : 8 * t + 8].astype(BF16)
    for t in range(3):
        ff_ref[8 + t] = d_ref[0, 8 * t : 8 * t + 8].astype(BF16)
    order = hidden_map(False).astype(BF16)
    for base, ref in ((2, g_ref), (5, u_ref)):
        w = (ref[0].astype(BF16).astype(F32) * gain2).astype(BF16).astype(F32)
        tall = jnp.concatenate([w[:, 384 * i : 384 * i + 384] for i in range(8)], 0).astype(BF16)
        tall = matmul(tall, order)
        for t in range(3):
            for i in range(8):
                ff_ref[base + t, :, 128 * i : 128 * i + 128] = tall[
                    8 * i : 8 * i + 8, 128 * t : 128 * t + 128
                ].astype(BF16)


def prepare(x, out_weight, gate, up, down, gain2):
    outs = [((UNITS, 8, WIDTH), BF16)] + [((ROWS, 512), BF16)] * 2
    return call(
        prepare_kernel, outs, (x, out_weight, gate, up, down, gain2), flops=10**7, nbytes=2 * MIB,
    )


def pack_heads_kernel(moves, own, gq_ref, gk_ref, q_ref, k_ref, v_ref, g1_ref, after, send_ref):
    moves.need()
    gain1 = column(g1_ref[...].astype(BF16).astype(F32))

    def scaled(ref):
        return (ref[0].astype(BF16).astype(F32) * gain1).astype(BF16)

    query = scaled(q_ref)
    key = scaled(k_ref)
    value = scaled(v_ref).astype(F32)
    value = jnp.concatenate([value[:, 128 * i : 128 * i + 128] for i in range(8)], 0).astype(BF16)
    value = matmul(value, channel_map(False).astype(BF16))
    spot = iota((8, SIZE), 1) == own[0]
    row = iota((8, SIZE), 0)
    gq = jnp.full((8, SIZE), gq_ref[0, 0], F32).astype(BF16).astype(F32)
    gk = jnp.full((8, SIZE), gk_ref[0, 0], F32).astype(BF16).astype(F32)
    gains = jnp.where(spot & (row == 0), gq, jnp.where(spot & (row == 1), gk, 0.0)).astype(BF16)
    for f in range(HEADS):
        h = f // 2
        tile = jnp.concatenate(
            [
                query[:, 128 * f : 128 * f + 128],
                key[:, 128 * h : 128 * h + 128],
                value[8 * h : 8 * h + 8].astype(BF16),
                gains,
            ],
            1,
        )
        send_ref[f] = tile


def pack_heads(own, gq, gk, q, k, v, g1, after):
    return call(
        pack_heads_kernel, [((HEADS, 8, 512), BF16)], (own, gq, gk, q, k, v, g1, after),
        scalars=(0, 1, 2), anywhere=(7,), flops=10**7, nbytes=2 * MIB,
    )[0]


def pack_rows_kernel(moves, q_ref, k_ref, v_ref, g1_ref, after, out_ref):
    moves.need()
    gain1 = column(g1_ref[...].astype(BF16).astype(F32))

    def scaled(w):
        return (w.astype(BF16).astype(F32) * gain1).astype(BF16)

    out_ref[0] = scaled(q_ref[0, :, :WIDTH])
    out_ref[1] = scaled(q_ref[0, :, WIDTH:])
    out_ref[2] = scaled(k_ref[0])
    value = scaled(v_ref[0]).astype(F32)
    value = jnp.concatenate([value[:, 128 * i : 128 * i + 128] for i in range(8)], 0).astype(BF16)
    value = matmul(value, channel_map(False).astype(BF16))
    for i in range(8):
        out_ref[3, :, 128 * i : 128 * i + 128] = value[8 * i : 8 * i + 8].astype(BF16)


def pack_rows(q, k, v, g1, after):
    return call(
        pack_rows_kernel, [((4, 8, WIDTH), BF16)], (q, k, v, g1, after), anywhere=(4,),
        flops=10**7, nbytes=MIB,
    )[0]


def row_limits(scal, first, shape, along):
    at = iota(shape, along)
    block, offset = at // ROWS, at % ROWS
    start = jnp.zeros(shape, jnp.int32)
    for i in range(4):
        start = jnp.where(block == i, scal[2 + first + i], start)
    return jnp.minimum(start + offset, scal[1] - 1)


def places(scal, part, late, early):
    first, second = scal[34 + part] ^ early, scal[35 - part] ^ late
    return 4 * first + second if part == 0 else 4 * second + first


def attend_kernel(moves, scal, *refs):
    tokens, (own_ref, other_ref, cos_ref, sin_ref) = (refs[:4], refs[4:8]), refs[8:12]
    o_ref, q_ref, k_ref, v_ref, lse_ref, p_ref, w_ref, kc, vc, va, acc, proj = refs[12:]
    total = scal[1]
    kc[...] = jnp.zeros_like(kc)
    vc[...] = jnp.zeros_like(vc)
    va[:, 128:] = jnp.ones((PLACES * ROWS, 128), BF16)
    moves.need(9, 10)
    for mask in range(4):
        for c, ref in enumerate((own_ref, other_ref)):
            block = 2 * (scal[36] ^ mask) + (scal[37] ^ c)
            w_ref[pl.ds(pl.multiple_of(ROWS * block, ROWS), ROWS), :] = ref[mask]
    moves.flush(6)
    for part in range(2):
        for late in range(4):
            moves.need(1 + 4 * part + late)
            w = w_ref[512 * part : 512 * part + 512, :384]
            out = matmul(tokens[part][late][...].reshape(4 * ROWS, 512), w)
            for early in range(4):
                e = places(scal, part, late, early)
                block = out[ROWS * early : ROWS * early + ROWS]
                if part == 0:
                    proj[e] = block
                else:
                    proj[e] += block
    moves.need()
    rows8 = iota((WIDTH, SIZE), 0) % 8
    gains = w_ref[:, 384:].astype(F32)
    query_gain = jnp.sum(jnp.where(rows8 == 0, gains, 0.0), 0, keepdims=True)
    key_gain = jnp.sum(jnp.where(rows8 == 1, gains, 0.0), 0, keepdims=True)
    for e in range(PLACES):
        block = proj[e]
        query, key = block[:, :128], block[:, 128:256]
        p_ref[e] = block[:, :256]
        cos, sin = cos_ref[e], sin_ref[e]
        query = query * mean_scale(query) * query_gain
        q_ref[e] = (query * cos + swap_halves(query) * sin).astype(BF16)
        key = key * mean_scale(key) * key_gain
        start = scal[2 + e]
        kc[pl.ds(start, ROWS), :] = key * cos + swap_halves(key) * sin
        vc[pl.ds(start, ROWS), :] = block[:, 256:]
    moves.flush(5)
    slots = PLACES * ROWS
    k_ref[...] = kc[:slots].astype(BF16)
    v_ref[...] = vc[:slots].astype(BF16)
    va[:, :128] = v_ref[...]
    moves.flush(1, 2, 3)

    for j in range(4):
        query = q_ref[4 * j : 4 * j + 4].reshape(512, SIZE)
        limit = row_limits(scal, 4 * j, (512, 512), 0)
        acc[...] = jnp.zeros_like(acc)

        def step(masked, query=query, limit=limit):
            def body(b, carry):
                at = pl.multiple_of(b * 512, 512)
                s = matmul_nt(query, k_ref[pl.ds(at, 512), :])
                prob = jnp.exp2(s * SCALE2)
                if masked:
                    prob = jnp.where(iota((512, 512), 1) + at <= limit, prob, 0.0)
                acc[...] += matmul(prob.astype(BF16), va[pl.ds(at, 512), :])
                return carry

            return body

        full = (scal[2 + 4 * j] + 1) // 512
        last = jnp.minimum(scal[2 + 4 * j + 3] + ROWS - 1, total - 1) // 512 + 1
        lax.fori_loop(0, full, step(False), 0)
        lax.fori_loop(full, last, step(True), 0)
        weight = acc[:, 128:]
        o_ref[4 * j : 4 * j + 4] = (
            (acc[:, :128] / weight).astype(BF16).reshape(4, ROWS, SIZE)
        )
        lse_ref[:, 512 * j : 512 * j + 512] = jnp.log2(weight).T[:8]


def attend(scal, tokens, weights, cos, sin):
    slots = PLACES * ROWS
    blocks = (PLACES, ROWS, SIZE)
    outs = [
        (blocks, BF16),
        (blocks, BF16),
        ((slots, SIZE), BF16),
        ((slots, SIZE), BF16),
        ((8, slots), F32),
        ((PLACES, ROWS, 256), F32),
        ((WIDTH, 512), BF16),
    ]
    scratch = [
        pltpu.VMEM((slots + ROWS, SIZE), F32),
        pltpu.VMEM((slots + ROWS, SIZE), F32),
        pltpu.VMEM((slots, 256), BF16),
        pltpu.VMEM((512, 256), F32),
        pltpu.VMEM((PLACES, ROWS, 384), F32),
    ]
    return call(
        attend_kernel, outs, (scal, *tokens, *weights, cos, sin), (0,), scratch=scratch,
        flops=5 * 10**9, nbytes=12 * MIB,
    )


def retreat_kernel(
    moves, scal, do_ref, o_ref, q_ref, k_ref, v_ref, lse_ref, after, dq, dk, dv, delta
):
    total = scal[1]
    moves.need()
    dk[...] = jnp.zeros_like(dk)
    dv[...] = jnp.zeros_like(dv)
    ones = jnp.ones((8, SIZE), F32)

    for j in range(4):
        query = q_ref[4 * j : 4 * j + 4].reshape(512, SIZE)
        grad = do_ref[4 * j : 4 * j + 4].reshape(512, SIZE)
        out = o_ref[4 * j : 4 * j + 4].reshape(512, SIZE)
        prod = grad.astype(F32) * out.astype(F32)
        delta[...] = lax.dot_general(
            ones, prod, (((1,), (1,)), ((), ())), preferred_element_type=F32,
            precision=lax.Precision.HIGHEST,
        )
        limit = row_limits(scal, 4 * j, (8, 512), 1)[:1]
        dq[j] = jnp.zeros((512, SIZE), F32)

        def step(masked, query=query, grad=grad, limit=limit, j=j):
            def body(b, carry):
                at = pl.multiple_of(b * 512, 512)
                key = k_ref[pl.ds(at, 512), :]
                s = matmul_nt(key, query)
                prob = jnp.exp2(s * SCALE2 - lse_ref[:1, 512 * j : 512 * j + 512])
                if masked:
                    prob = jnp.where(iota((512, 512), 0) + at <= limit, prob, 0.0)
                dv[pl.ds(at, 512), :] += matmul(prob.astype(BF16), grad)
                prob_grad = matmul_nt(v_ref[pl.ds(at, 512), :], grad)
                score = (prob * (prob_grad - delta[:1])).astype(BF16)
                dk[pl.ds(at, 512), :] += matmul(score, query)
                dq[j] += matmul_tn(score, key)
                return carry

            return body

        full = (scal[2 + 4 * j] + 1) // 512
        last = jnp.minimum(scal[2 + 4 * j + 3] + ROWS - 1, total - 1) // 512 + 1
        lax.fori_loop(0, full, step(False), 0)
        lax.fori_loop(full, last, step(True), 0)


def retreat(scal, head_grad, saved, after):
    outs = [((4, 512, SIZE), F32)] + [((PLACES * ROWS + ROWS, SIZE), F32)] * 2
    return call(
        retreat_kernel, outs, (scal, head_grad, *saved, after), (0,), (7,),
        scratch=[pltpu.VMEM((8, 512), F32)], flops=8 * 10**9, nbytes=6 * MIB,
    )


def project_kernel(
    moves, scal, w_ref, cos_ref, sin_ref, p_ref, dq, dk, dv, after, low, gains_ref
):
    moves.need()
    rows8 = iota((WIDTH, SIZE), 0) % 8
    gains = w_ref[:, 384:].astype(F32)
    query_gain = jnp.sum(jnp.where(rows8 == 0, gains, 0.0), 0, keepdims=True)
    key_gain = jnp.sum(jnp.where(rows8 == 1, gains, 0.0), 0, keepdims=True)

    query_part = jnp.zeros((1, SIZE), F32)
    key_part = jnp.zeros((1, SIZE), F32)

    def head(grad, projected, gain, cos, sin):
        turned = grad * cos - swap_halves(grad) * sin
        scale = mean_scale(projected)
        normal = projected * scale
        part = jnp.sum(turned * normal, 0, keepdims=True)
        return norm_back(turned * gain, normal, scale).astype(BF16), part

    for e in range(PLACES):
        cos, sin = cos_ref[e], sin_ref[e]
        at = ROWS * (e % 4)
        query_grad = dq[e // 4, at : at + ROWS, :] * SCALE
        low[e, :, :128], part = head(query_grad, p_ref[e, :, :128], query_gain, cos, sin)
        query_part += part
        live = iota((ROWS, SIZE), 0) < scal[18 + e]
        start = scal[2 + e]
        key_grad = jnp.where(live, dk[pl.ds(start, ROWS), :], 0.0) * SCALE
        low[e, :, 128:256], part = head(key_grad, p_ref[e, :, 128:], key_gain, cos, sin)
        key_part += part
        low[e, :, 256:] = jnp.where(live, dv[pl.ds(start, ROWS), :], 0.0).astype(BF16)

    gains_ref[...] = jnp.where(iota((8, SIZE), 0) == 0, query_part, key_part)


def project(scal, weight, cos, sin, projected, grads, after):
    outs = [((PLACES, ROWS, 384), BF16), ((8, SIZE), F32)]
    return call(
        project_kernel, outs, (scal, weight, cos, sin, projected, *grads, after), (0,), (8,),
        flops=10**8, nbytes=10 * MIB,
    )


def weigh_heads_kernel(moves, scal, *refs):
    tokens, (low, gains_ref, mine_ref, theirs_ref, grad) = (refs[:4], refs[4:8]), refs[8:]
    moves.need()
    for part in range(2):
        total = jnp.zeros((512, 384), F32)
        for late in range(4):
            rows = jnp.concatenate([low[places(scal, part, late, early)] for early in range(4)], 0)
            total += matmul_tn(tokens[part][late][...].reshape(4 * ROWS, 512), rows)
        grad[512 * part : 512 * part + 512, :384] = total.astype(BF16)
    rows8 = iota((WIDTH, SIZE), 0) % 8
    spot = iota((WIDTH, SIZE), 0) // 8 == iota((WIDTH, SIZE), 1)
    extra = jnp.where(rows8 == 0, gains_ref[:1], jnp.where(rows8 == 1, gains_ref[1:2], 0.0))
    grad[:, 384:] = jnp.where(spot, extra, 0.0).astype(BF16)
    for x in range(4):
        for c, ref in enumerate((mine_ref, theirs_ref)):
            block = 2 * x + (scal[37] ^ c)
            ref[x] = grad[pl.ds(pl.multiple_of(ROWS * block, ROWS), ROWS), :]


def weigh_heads(scal, tokens, low, gains):
    return call(
        weigh_heads_kernel, [((4, ROWS, 512), BF16)] * 2, (scal, *tokens, low, gains), (0,),
        scratch=[pltpu.VMEM((WIDTH, 512), BF16)], flops=2 * 10**9, nbytes=7 * MIB,
    )


def feed_kernel(
    moves, scal, mixed_ref, x_ref, cot_ref, ff_ref,
    out_ref, mg_ref, send_ref, mine_ref, theirs_ref, right_ref,
    w, sems, gate, up, half, normal,
):
    core, count = scal[0], scal[1]
    copies = [pltpu.make_async_copy(ff_ref.at[u], w.at[u], sems.at[u]) for u in range(UNITS)]
    for copy in copies:
        copy.start()

    def left(unit, value):
        even = jnp.concatenate([value[:, 256 * i : 256 * i + 128] for i in range(4)], 1)
        odd = jnp.concatenate([value[:, 256 * i + 128 : 256 * i + 256] for i in range(4)], 1)
        at = pl.ds(512 * unit, 512) if isinstance(unit, int) else pl.ds(pl.multiple_of(512 * unit, 512), 512)

        @pl.when(core == 0)
        def _():
            mine_ref[:, at] = even
            theirs_ref[:, at] = odd

        @pl.when(core == 1)
        def _():
            mine_ref[:, at] = odd
            theirs_ref[:, at] = even

    low_lanes = iota((ROWS, SIZE), 1) < 64
    moves.need()
    for i in range(8):
        a, b = mixed_ref[2 * i].astype(F32), mixed_ref[2 * i + 1].astype(F32)
        at = slice(128 * i, 128 * i + 128)
        half[0, :, at] = jnp.where(low_lanes, a, swap_halves(b)).astype(BF16)
        half[1, :, at] = jnp.where(low_lanes, swap_halves(a), b).astype(BF16)
    out_ref[...] = x_ref[...]
    for t in range(2):
        left(t, half[t])
        copies[t].wait()
        out_ref[...] += matmul(half[t], w[t])
    middle = out_ref[...]
    scale = mean_scale(middle)
    normal[...] = middle * scale
    normal_low = normal[...].astype(BF16)
    left(2, normal_low)
    live = iota((ROWS, 1), 0) < count
    branch = jnp.where(live, cot_ref[...], 0.0).astype(BF16)
    right_ref[:, 7 * WIDTH :] = branch
    mg_ref[...] = jnp.zeros_like(mg_ref)
    for t in range(3):
        copies[2 + t].wait()
        copies[5 + t].wait()
        copies[8 + t].wait()
        gate[...] = matmul(normal_low, w[2 + t])
        up[...] = matmul(normal_low, w[5 + t])
        g, u = gate[...], up[...]
        sig = 1.0 / (1.0 + jnp.exp(-g))
        inner = (g * sig * u).astype(BF16)
        left(3 + t, inner)
        out_ref[...] += matmul(inner, w[8 + t])
        grad_inner = matmul_nt(branch, w[8 + t])
        gate_grad = (grad_inner * u * sig * (1.0 + g * (1.0 - sig))).astype(BF16)
        up_grad = (grad_inner * g * sig).astype(BF16)
        right_ref[:, WIDTH * (1 + t) : WIDTH * (2 + t)] = gate_grad
        right_ref[:, WIDTH * (4 + t) : WIDTH * (5 + t)] = up_grad
        mg_ref[...] += matmul_nt(gate_grad, w[2 + t])
        mg_ref[...] += matmul_nt(up_grad, w[5 + t])
    middle_grad = jnp.where(live, cot_ref[...], 0.0) + norm_back(mg_ref[...], normal[...], scale)
    mg_ref[...] = middle_grad
    attn_grad = middle_grad.astype(BF16)
    right_ref[:, :WIDTH] = attn_grad
    first = matmul_nt(attn_grad, w[0])
    second = matmul_nt(attn_grad, w[1])
    for i in range(8):
        a, b = first[:, 128 * i : 128 * i + 128], second[:, 128 * i : 128 * i + 128]
        send_ref[2 * i] = jnp.where(low_lanes, a, swap_halves(b)).astype(BF16)
        send_ref[2 * i + 1] = jnp.where(low_lanes, swap_halves(a), b).astype(BF16)


def feed(scal, mixed, x, cotangent, ff):
    outs = [
        ((ROWS, WIDTH), F32),
        ((ROWS, WIDTH), F32),
        ((HEADS, ROWS, SIZE), BF16),
        ((ROWS, 3072), BF16),
        ((ROWS, 3072), BF16),
        ((ROWS, 8 * WIDTH), BF16),
    ]
    scratch = [
        pltpu.VMEM((UNITS, WIDTH, WIDTH), BF16),
        pltpu.SemaphoreType.DMA((UNITS,)),
        pltpu.VMEM((ROWS, WIDTH), F32),
        pltpu.VMEM((ROWS, WIDTH), F32),
        pltpu.VMEM((2, ROWS, WIDTH), BF16),
        pltpu.VMEM((ROWS, WIDTH), F32),
    ]
    return call(
        feed_kernel, outs, (scal, mixed, x, cotangent, ff), (0,), (4,), scratch=scratch,
        flops=6 * 10**9, nbytes=28 * MIB,
    )


def weigh_kernel(moves, scal, lm_ref, lt_ref, rm_ref, rt_ref, after, *refs):
    outs, (left, right), buffers = refs[:8], refs[8:10], refs[10:]
    moves.need(1, 2)
    for l in range(6):
        at = slice(512 * l, 512 * l + 512)
        left[at, :128] = lm_ref[:, at].astype(F32).T.astype(BF16)
        left[at, 128:] = lt_ref[:, at].astype(F32).T.astype(BF16)
    moves.need()
    right[:128] = rm_ref[...]
    right[128:] = rt_ref[...]
    for s, (part, mode, halves) in enumerate(QUARTERS):
        buffer = buffers[s]
        for n, (unit, c) in enumerate(halves):
            l, r = PAIRS[unit]
            at = WIDTH * r + 512 * c
            out = matmul(left[512 * l : 512 * l + 512], right[:, at : at + 512])
            for i in range(4):
                if part == 0:
                    block = out[128 * i : 128 * i + 128]
                else:
                    rows = [128 * x + 32 * i for x in range(4)]
                    block = jnp.concatenate([out[r : r + 32] for r in rows], 0)
                buffer[i, n] = block.astype(BF16)
        for i, mask in enumerate(KEPT[mode]):
            moves.push(buffer.at[scal[part] ^ mask], outs[2 * s + i // 2].at[i % 2])


def weigh(scal, mine, theirs, right, right_theirs, after):
    outs = [((2, len(h), 128, 512), BF16) for p, m, h in QUARTERS for i in range(2)]
    scratch = [pltpu.VMEM((3072, 256), BF16), pltpu.VMEM((256, 8 * WIDTH), BF16)]
    scratch += [pltpu.VMEM((4, len(h), 128, 512), BF16) for p, m, h in QUARTERS]
    out = call(
        weigh_kernel, outs, (scal, mine, theirs, right, right_theirs, after), (0,), (5,), range(8),
        scratch, flops=3 * 10**9, nbytes=18 * MIB, sends=16,
    )
    return out[::2], out[1::2]


AXES = ("x", "y", "z")


def add(a, b):
    return a.astype(F32) + b.astype(F32)


def four(refs):
    return add(refs[0][...], refs[1][...]) + add(refs[2][...], refs[3][...])


def add_first_kernel(moves, *refs):
    keeps, gots, (after,), new_keeps, new_sends = refs[:4], refs[4:8], refs[8:9], refs[9:13], refs[13:]
    for s in range(4):
        moves.need(s, 4 + s)
        new_sends[s][...] = add(keeps[s][1], gots[s][1]).astype(BF16)
        moves.flush(4 + s)
        new_keeps[s][...] = add(keeps[s][0], gots[s][0]).astype(BF16)
        moves.flush(s)


def add_first(keeps, gots, after):
    outs = [(k.shape[1:], BF16) for k in keeps] * 2
    out = call(
        add_first_kernel, outs, (*keeps, *gots, after), anywhere=(8,), flops=10**7, nbytes=17 * MIB
    )
    return out[:4], out[4:]


PART_ROWS = 32 * len(PARTS[0])


def join_kernel(moves, scal, *refs):
    keeps, gots, (mine_ref, theirs_ref), outs, buffers = refs[:4], refs[4:8], refs[8:10], refs[10:18], refs[18:]
    for s, (part, mode, halves) in enumerate(QUARTERS):
        moves.need(1 + s, 5 + s)
        first = 32 * 6 * mode
        for n in range(len(halves)):
            total = add(keeps[s][n], gots[s][n])
            for i in range(4):
                at = first + 32 * n
                buffers[part][i, at : at + 32] = total[32 * i : 32 * i + 32].astype(BF16)
        if s == 1:
            for mask in range(4):
                moves.push(buffers[0].at[scal[1] ^ mask], outs[mask])
    moves.need()
    for x in range(4):
        buffers[1][x, PART_ROWS:] = add(mine_ref[x], theirs_ref[x]).astype(BF16)
    for mask in range(4):
        moves.push(buffers[1].at[scal[0] ^ mask], outs[4 + mask])


def join(scal, keeps, gots, mine, theirs):
    shapes = [(PART_ROWS, 512), (PART_ROWS + ROWS, 512)]
    outs = [(shape, BF16) for shape in shapes for mask in range(4)]
    scratch = [pltpu.VMEM((4, *shape), BF16) for shape in shapes]
    return call(
        join_kernel, outs, (scal, *keeps, *gots, mine, theirs), (0,), (), range(8), scratch,
        flops=10**7, nbytes=10 * MIB, sends=8,
    )


def pass_on_kernel(moves, scal, *refs):
    got, outs, heads_ref, buffer = refs[:8], refs[8:12], refs[12], refs[13]
    for part in (1, 0):
        moves.need(*range(1 + 4 * part, 5 + 4 * part))
        total = four(got[4 * part : 4 * part + 4])
        if part == 1:
            for f in range(HEADS):
                at = PART_ROWS + 8 * f
                heads_ref[f] = total[at : at + 8].astype(BF16)
            moves.flush(4)
        for n in range(11):
            for i in range(4):
                at = 88 * part + 8 * n
                buffer[i, at : at + 8] = total[32 * n + 8 * i : 32 * n + 8 * i + 8].astype(BF16)
    for mask in range(4):
        moves.push(buffer.at[scal[2] ^ mask], outs[mask])


def pass_on(scal, got):
    outs = [((176, 512), BF16)] * 4 + [((HEADS, 8, 512), BF16)]
    out = call(
        pass_on_kernel, outs, (scal, *got), (0,), raw=range(4),
        scratch=[pltpu.VMEM((4, 176, 512), BF16)], flops=10**7, nbytes=5 * MIB, sends=4,
    )
    return out[:4], out[4]


def finish_heads_kernel(
    moves, back_ref, q_ref, k_ref, v_ref, g1_ref, dq_ref, dk_ref, dv_ref, dg_ref, dqk_ref
):
    moves.need()
    gain = column(g1_ref[...].astype(BF16).astype(F32))
    order = channel_map(True)
    dg = jnp.zeros((8, 1), F32)
    extra = jnp.zeros((8, SIZE), F32)
    for h in range(KV_HEADS):
        pair = []
        for f in (2 * h, 2 * h + 1):
            total = back_ref[f].astype(F32)
            at = slice(128 * f, 128 * f + 128)
            dq_ref[0, :, at] = total[:, :128] * gain
            w = q_ref[0, :, at].astype(BF16).astype(F32)
            dg += jnp.sum(total[:, :128] * w, 1, keepdims=True)
            extra += total[:, 384:]
            pair.append(total)
        at = slice(128 * h, 128 * h + 128)
        both = pair[0] + pair[1]
        dk = both[:, 128:256]
        dv = exact(both[:, 256:384], order)
        dk_ref[0, :, at] = dk * gain
        dv_ref[0, :, at] = dv * gain
        dg += jnp.sum(dk * k_ref[0, :, at].astype(BF16).astype(F32), 1, keepdims=True)
        dg += jnp.sum(dv * v_ref[0, :, at].astype(BF16).astype(F32), 1, keepdims=True)
    dg_ref[...] = jnp.sum(jnp.where(iota((8, 8), 0) == iota((8, 8), 1), dg, 0.0), 0, keepdims=True)
    dqk_ref[...] = jnp.broadcast_to(jnp.sum(extra, 1, keepdims=True), (8, SIZE))


def finish_heads(back, q, k, v, g1):
    outs = [((1, 8, 2048), F32), ((1, 8, 1024), F32), ((1, 8, 1024), F32), ((1, 8), F32), ((8, SIZE), F32)]
    return call(finish_heads_kernel, outs, (back, q, k, v, g1), flops=10**7, nbytes=3 * MIB)


def finish_feed_kernel(moves, *refs):
    got, (g_ref, u_ref, g2_ref), outs = refs[:4], refs[4:7], refs[7:]
    do_ref, dg_ref, du_ref, dd_ref, gain_ref = outs
    moves.need()
    total = four(got)
    tiles = {key: total[8 * n : 8 * n + 8] for n, key in enumerate(HALVES)}
    units = [jnp.concatenate([tiles[u, 0], tiles[u, 1]], 1) for u in range(UNITS)]
    for t in range(2):
        do_ref[0, 8 * t : 8 * t + 8] = units[t]
    for t in range(3):
        dd_ref[0, 8 * t : 8 * t + 8] = units[8 + t]
    gain = column(g2_ref[...].astype(BF16).astype(F32))
    order = hidden_map(True)
    dg = jnp.zeros((8, 1), F32)
    for base, w_ref, out_ref in ((2, g_ref, dg_ref), (5, u_ref, du_ref)):
        tall = jnp.concatenate(
            [
                jnp.concatenate([units[base + t][:, 128 * i : 128 * i + 128] for t in range(3)], 1)
                for i in range(8)
            ],
            0,
        )
        tall = exact(tall, order)
        for i in range(8):
            at = slice(384 * i, 384 * i + 384)
            grad = tall[8 * i : 8 * i + 8]
            dg += jnp.sum(grad * w_ref[0, :, at].astype(BF16).astype(F32), 1, keepdims=True)
            out_ref[0, :, at] = grad * gain
    gain_ref[...] = jnp.sum(jnp.where(iota((8, 8), 0) == iota((8, 8), 1), dg, 0.0), 0, keepdims=True)


def finish_feed(got, gate, up, g2):
    outs = [
        ((1, 16, 1024), F32), ((1, 8, 3072), F32), ((1, 8, 3072), F32), ((1, 24, 1024), F32), ((1, 8), F32),
    ]
    return call(finish_feed_kernel, outs, (*got, gate, up, g2), flops=10**8, nbytes=3 * MIB)


def finish_input_kernel(moves, low_ref, w_ref, x_ref, mg_ref, out_ref):
    moves.need(0)
    halves = [
        jnp.concatenate([low_ref[8 * i + h, :, :128] for h in range(8)], 1) for i in range(2)
    ]
    for at in (slice(128, 256), slice(256, 384)):
        pairs = [add(low_ref[2 * h, :, at], low_ref[2 * h + 1, :, at]) for h in range(8)]
        halves.append(jnp.concatenate(pairs, 1).astype(BF16))
    moves.need(1)
    out_ref[...] = matmul_nt(halves[0], w_ref[0])
    for i in range(1, 4):
        out_ref[...] += matmul_nt(halves[i], w_ref[i])
    moves.need()
    x = x_ref[...]
    scale = mean_scale(x)
    out_ref[...] = mg_ref[...] + norm_back(out_ref[...], x * scale, scale)


def finish_input(low, weights, x, middle_grad):
    return call(
        finish_input_kernel, [((ROWS, WIDTH), F32)], (low, weights, x, middle_grad),
        flops=10**9, nbytes=11 * MIB,
    )[0]


def other(v):
    return lax.ppermute(v, "core", [(0, 1), (1, 0)])


def trade(v, axes):
    return lax.all_to_all(v, axes, split_axis=0, concat_axis=0, tiled=True)


def swap(terms, axis):
    return [terms[0]] + [
        lax.ppermute(terms[mask], axis, [(i, i ^ mask) for i in range(4)]) for mask in (1, 3, 2)
    ]


def in_order(v):
    return [v[0], v[1], v[3], v[2]]


def shards(
    block_input, counts, query_weight, key_matrix, value_matrix, out_weight, gate_weight,
    up_weight, down_weight, attn_gain, mlp_gain, query_gain, key_gain, cotangent,
):
    place = lax.axis_index(TOKENS)
    group = lax.axis_index(("x", "core"))
    core = lax.axis_index("core")
    own = lax.axis_index(ALL).reshape(1).astype(jnp.int32)
    ff_pack, early, late = prepare(
        block_input, out_weight, gate_weight, up_weight, down_weight, mlp_gain
    )
    ff = lax.all_gather(ff_pack, ALL, axis=1, tiled=True)
    blocks = [swap([early] * 4, "y"), swap([late] * 4, "z")]
    head_send = pack_heads(
        own, query_gain, key_gain, query_weight, key_matrix, value_matrix, attn_gain, ff_pack
    )
    head_weights = jnp.stack(in_order(swap([trade(head_send, TOKENS).reshape(ROWS, 512)] * 4, "x")))
    head_weights = (head_weights, other(head_weights))
    blocks = [jnp.stack(in_order(b)) for b in blocks]
    tokens = []
    for block, axis in zip(blocks, "zy"):
        tokens += in_order(swap([block] * 4, axis))

    group_counts = lax.dynamic_index_in_dim(counts, group, 0, keepdims=False)
    starts = jnp.cumsum(group_counts) - group_counts
    own_count = lax.dynamic_index_in_dim(group_counts, place, 0, keepdims=False)
    scal = jnp.concatenate(
        [place.reshape(1), jnp.sum(group_counts).reshape(1), starts, group_counts]
        + [lax.axis_index(a).reshape(1) for a in ("y", "z", "x", "core")]
    ).astype(jnp.int32)
    inverse = ROPE_BASE ** (-(jnp.arange(64, dtype=F32) * 2.0 / SIZE))
    position = starts[:, None] + jnp.arange(ROWS, dtype=jnp.int32)[None, :]
    angles = position.astype(F32)[:, :, None] * inverse
    cosine, sine = jnp.cos(angles), jnp.sin(angles)
    cos = jnp.concatenate([cosine, cosine], -1)
    sin = jnp.concatenate([-sine, sine], -1)

    mixed_head, *saved, projected, head_weight = attend(scal, tokens, head_weights, cos, sin)
    rows = pack_rows(query_weight, key_matrix, value_matrix, attn_gain, mixed_head)
    rows = lax.all_gather(rows, ALL, axis=1, tiled=True)
    mixed = trade(mixed_head, TOKENS)
    block_output, middle_grad, grad_send, mine, theirs, right = feed(
        jnp.stack([core, own_count]).astype(jnp.int32), mixed, block_input, cotangent, ff
    )
    head_grad = trade(grad_send, TOKENS)

    chip = jnp.stack([lax.axis_index(a) for a in AXES]).astype(jnp.int32)
    keeps, sends = weigh(chip, mine, other(theirs), right, other(right), head_grad)

    def step(sends, order):
        return [
            lax.ppermute(v, ORDERS[part][0], [(i, i ^ MASKS[mode][order]) for i in range(4)])
            for v, (part, mode, halves) in zip(sends, QUARTERS)
        ]

    gots = step(sends, 0)
    grads = retreat(scal, head_grad, [mixed_head] + saved, sends[0])
    keeps, sends = add_first(keeps, gots, grads[0])
    gots = step(sends, 1)
    low, head_gains = project(scal, head_weight, cos, sin, projected, grads, sends[0])
    token_low = trade(low, TOKENS)
    head_mine, head_theirs = weigh_heads(scal, tokens, low, head_gains)
    terms = join(chip, keeps, gots, head_mine, other(head_theirs))
    terms, head_terms = pass_on(chip, swap(terms[:4], "y") + swap(terms[4:], "x"))
    got = swap(terms, "z")
    head_back = trade(head_terms, TOKENS)
    input_grad = finish_input(token_low, rows, block_input, middle_grad)
    query_grad, key_grad, value_grad, attn_gain_grad, head_gains = finish_heads(
        head_back, query_weight, key_matrix, value_matrix, attn_gain
    )
    out_grad, gate_grad, up_grad, down_grad, mlp_gain_grad = finish_feed(
        got, gate_weight, up_weight, mlp_gain
    )
    return (
        block_output,
        input_grad,
        query_grad,
        key_grad,
        value_grad,
        out_grad,
        gate_grad,
        up_grad,
        down_grad,
        attn_gain_grad,
        mlp_gain_grad,
        head_gains[0:1, 0:1],
        head_gains[1:2, 0:1],
    )


def solution(mesh):
    fine = Mesh(mesh.devices.reshape(4, 2, 4, 4), ALL)
    tokens = P(ALL, None)
    weight = P(None, ALL, None)
    gain = P(None, ALL)
    return jax.shard_map(
        shards,
        mesh=fine,
        in_specs=(tokens, P()) + (weight,) * 7 + (gain,) * 4 + (tokens,),
        out_specs=(tokens, tokens) + (weight,) * 7 + (gain,) * 4,
        check_vma=False,
    )
```

```python
import functools

import jax
import jax.numpy as jnp
from jax import lax
from jax.experimental import pallas as pl
from jax.experimental.pallas import tpu as pltpu
from jax.sharding import Mesh, PartitionSpec as P

HEADS = 16
KV_HEADS = 8
SIZE = 128
WIDTH = 1024
ROWS = 128
PLACES = 16
EPSILON = 1e-06
ROPE_BASE = 1000000.0
SCALE = SIZE**-0.5
SCALE2 = SCALE * 1.4426950408889634
F32 = jnp.float32
BF16 = jnp.bfloat16
MIB = 1 << 20
US = 3_600_000

TOKENS = ("y", "z")
ALL = ("x", "core", "y", "z")

UNITS = 11
HALVES = [(u, c) for u in range(UNITS) for c in range(2)]
PARTS = [HALVES[:9], HALVES[9:18], HALVES[18:]]
FIRST = ("x", "y", "z")
MASKS = ((1, 3), (3, 1))
KEPT = ((0, 3, 1, 2), (0, 1, 3, 2))
SEEN = ((0, 1, 3, 2), (0, 3, 1, 2))
QUARTERS = [
    (0, 0, PARTS[0][:5]), (0, 1, PARTS[0][5:]), (1, 0, PARTS[1][:5]), (1, 1, PARTS[1][5:]), (2, 0, PARTS[2]),
]
PAIRS = [(0, 0), (1, 0)] + [(2, 1 + t) for t in range(6)] + [(3 + t, 7) for t in range(3)]


def matmul(a, b):
    return lax.dot_general(a, b, (((1,), (0,)), ((), ())), preferred_element_type=F32)


def matmul_nt(a, b):
    return lax.dot_general(a, b, (((1,), (1,)), ((), ())), preferred_element_type=F32)


def matmul_tn(a, b):
    return lax.dot_general(a, b, (((0,), (0,)), ((), ())), preferred_element_type=F32)


def exact(a, b):
    return lax.dot_general(
        a, b, (((1,), (0,)), ((), ())), preferred_element_type=F32, precision=lax.Precision.HIGHEST
    )


SMEM = pl.BlockSpec(memory_space=pltpu.SMEM)
HBM = pl.BlockSpec(memory_space=pltpu.HBM)
VMEM = pl.BlockSpec(memory_space=pltpu.VMEM)


class Moves:
    def __init__(self, ins, outs, sems):
        self.ins, self.outs, self.sems, self.sent, self.pushed = ins, outs, sems, [], 0

    def need(self, *which):
        for i in which or list(self.ins):
            if i in self.ins:
                self.ins.pop(i).wait()

    def flush(self, *which):
        for i in which or list(self.outs):
            if i in self.outs:
                copy = self.outs.pop(i)
                copy.start()
                self.sent.append(copy)

    def push(self, source, target):
        copy = pltpu.make_async_copy(source, target, self.sems.at[self.pushed])
        copy.start()
        self.sent.append(copy)
        self.pushed += 1

    def finish(self):
        self.need()
        self.flush()
        for copy in self.sent:
            copy.wait()


def call(
    kernel, outs, args, scalars=(), anywhere=(), raw=(), scratch=(), limit=60, micros=1, sends=0, order=None, still=()
):
    moved = [i for i in range(len(args)) if i not in (*scalars, *anywhere, *still)]
    made = [i for i in range(len(outs)) if i not in raw]
    count, total = len(args), len(outs)

    def body(*refs):
        ins, out, rest = list(refs[:count]), list(refs[count : count + total]), list(refs[count + total :])
        here = [rest.pop(0) for i in moved]
        there = [rest.pop(0) for i in made]
        sems_in, sems_out = rest.pop(0), rest.pop(0)
        copies_in = {i: pltpu.make_async_copy(ins[i], here[n], sems_in.at[n]) for n, i in enumerate(moved)}
        copies_out = {
            i: pltpu.make_async_copy(there[n], out[i], sems_out.at[sends + n]) for n, i in enumerate(made)
        }
        for i in order or moved:
            copies_in[i].start()
        for n, i in enumerate(moved):
            ins[i] = here[n]
        for n, i in enumerate(made):
            out[i] = there[n]
        moves = Moves(copies_in, copies_out, sems_out)
        kernel(moves, *ins, *out, *rest)
        moves.finish()

    buffers = [pltpu.VMEM(args[i].shape, args[i].dtype) for i in moved]
    buffers += [pltpu.VMEM(*outs[i]) for i in made]
    sems = [pltpu.SemaphoreType.DMA((max(len(moved), 1),)), pltpu.SemaphoreType.DMA((len(made) + sends,))]
    return pl.pallas_call(
        body,
        out_shape=[jax.ShapeDtypeStruct(s, t) for s, t in outs],
        in_specs=[SMEM if i in scalars else VMEM if i in still else HBM for i in range(count)],
        out_specs=[HBM] * total,
        scratch_shapes=buffers + sems + list(scratch),
        compiler_params=pltpu.CompilerParams(vmem_limit_bytes=limit * MIB),
        cost_estimate=pl.CostEstimate(flops=0, bytes_accessed=US * micros, transcendentals=0),
    )(*args)


def iota(shape, dim):
    return lax.broadcasted_iota(jnp.int32, shape, dim)


def mean_scale(v):
    return lax.rsqrt(jnp.mean(v * v, -1, keepdims=True) + EPSILON)


def norm_back(grad, normal, scale):
    return scale * (grad - normal * jnp.mean(grad * normal, -1, keepdims=True))


def swap_halves(v):
    return pltpu.roll(v, 64, 1)


def column(row):
    return jnp.sum(jnp.where(iota((8, 8), 0) == iota((8, 8), 1), row, 0.0), 1, keepdims=True)


def hidden_map(back):
    shape = (384, 384)
    source, target = (iota(shape, 1), iota(shape, 0)) if back else (iota(shape, 0), iota(shape, 1))
    i, rest = source // 24, source % 24
    return jnp.where((rest // 8) * 128 + i * 8 + rest % 8 == target, 1.0, 0.0)


def channel_map(back):
    shape = (128, 128)
    source, target = (iota(shape, 1), iota(shape, 0)) if back else (iota(shape, 0), iota(shape, 1))
    i, rest = source // 16, source % 16
    return jnp.where((rest // 8) * 64 + i * 8 + rest % 8 == target, 1.0, 0.0)


def pack_feed_kernel(moves, o_ref, g_ref, u_ref, d_ref, g2_ref, ff_ref):
    moves.need()
    gain2 = column(g2_ref[...].astype(BF16).astype(F32))
    for t in range(2):
        ff_ref[t] = o_ref[0, 8 * t : 8 * t + 8].astype(BF16)
    for t in range(3):
        ff_ref[8 + t] = d_ref[0, 8 * t : 8 * t + 8].astype(BF16)
    order = hidden_map(False).astype(BF16)
    for base, ref in ((2, g_ref), (5, u_ref)):
        w = (ref[0].astype(BF16).astype(F32) * gain2).astype(BF16).astype(F32)
        tall = jnp.concatenate([w[:, 384 * i : 384 * i + 384] for i in range(8)], 0).astype(BF16)
        tall = matmul(tall, order)
        for t in range(3):
            for i in range(8):
                ff_ref[base + t, :, 128 * i : 128 * i + 128] = tall[
                    8 * i : 8 * i + 8, 128 * t : 128 * t + 128
                ].astype(BF16)


def pack_feed(out_weight, gate, up, down, gain2):
    outs = [((UNITS, 8, WIDTH), BF16)]
    return call(pack_feed_kernel, outs, (out_weight, gate, up, down, gain2), micros=2)[0]


def prepare_kernel(moves, x_ref, after, n0_ref, n1_ref):
    moves.need()
    x = x_ref[...]
    normal = (x * mean_scale(x)).astype(BF16)
    n0_ref[...] = normal[:, :512]
    n1_ref[...] = normal[:, 512:]


def prepare(x, after):
    return call(prepare_kernel, [((ROWS, 512), BF16)] * 2, (x, after), anywhere=(1,), micros=1)


def pack_heads_kernel(moves, own, gq_ref, gk_ref, q_ref, k_ref, v_ref, g1_ref, after, send_ref):
    moves.need()
    gain1 = column(g1_ref[...].astype(BF16).astype(F32))

    def scaled(ref):
        return (ref[0].astype(BF16).astype(F32) * gain1).astype(BF16)

    query = scaled(q_ref)
    key = scaled(k_ref)
    value = scaled(v_ref).astype(F32)
    value = jnp.concatenate([value[:, 128 * i : 128 * i + 128] for i in range(8)], 0).astype(BF16)
    value = matmul(value, channel_map(False).astype(BF16))
    spot = iota((8, SIZE), 1) == own[0]
    row = iota((8, SIZE), 0)
    gq = jnp.full((8, SIZE), gq_ref[0, 0], F32).astype(BF16).astype(F32)
    gk = jnp.full((8, SIZE), gk_ref[0, 0], F32).astype(BF16).astype(F32)
    gains = jnp.where(spot & (row == 0), gq, jnp.where(spot & (row == 1), gk, 0.0)).astype(BF16)
    for f in range(HEADS):
        h = f // 2
        tile = jnp.concatenate(
            [
                query[:, 128 * f : 128 * f + 128],
                key[:, 128 * h : 128 * h + 128],
                value[8 * h : 8 * h + 8].astype(BF16),
                gains,
            ],
            1,
        )
        send_ref[f] = tile


def pack_heads(own, gq, gk, q, k, v, g1, after):
    return call(
        pack_heads_kernel, [((HEADS, 8, 512), BF16)], (own, gq, gk, q, k, v, g1, after),
        scalars=(0, 1, 2), anywhere=(7,), micros=2,
    )[0]


def row_limits(scal, first, shape, along):
    at = iota(shape, along)
    block, offset = at // ROWS, at % ROWS
    start = jnp.zeros(shape, jnp.int32)
    for i in range(4):
        start = jnp.where(block == i, scal[2 + first + i], start)
    return jnp.minimum(start + offset, scal[1] - 1)


def places(scal, part, late, early):
    first, second = scal[34 + part] ^ early, scal[35 - part] ^ late
    return 4 * first + second if part == 0 else 4 * second + first


def attend_kernel(moves, scal, *refs):
    tokens, (own_ref, other_ref, cos_ref, sin_ref) = refs[:8], refs[8:12]
    o_ref, q_ref, k_ref, v_ref, lse_ref, p_ref, w_ref, kc, vc, va, acc, proj = refs[12:]
    total = scal[1]
    kc[...] = jnp.zeros_like(kc)
    vc[...] = jnp.zeros_like(vc)
    va[:, 128:] = jnp.ones((PLACES * ROWS, 128), BF16)
    moves.need(9, 10)
    for mask in range(4):
        for c, ref in enumerate((own_ref, other_ref)):
            block = 2 * (scal[36] ^ mask) + (scal[37] ^ c)
            w_ref[pl.ds(pl.multiple_of(ROWS * block, ROWS), ROWS), :] = ref[mask]
    moves.flush(6)
    for quarter in range(4):
        part, mode = divmod(quarter, 2)
        w = w_ref[256 * quarter : 256 * quarter + 256, :384]
        for half in range(2):
            moves.need(1 + 2 * quarter + half)
            rows = tokens[2 * quarter + half][...].reshape(8 * ROWS, 256)
            out = matmul(rows, w)
            for i in range(8):
                e = places(scal, part, SEEN[mode][2 * half + i // 4], i % 4)
                block = out[ROWS * i : ROWS * i + ROWS]
                if quarter == 0:
                    proj[e] = block
                else:
                    proj[e] += block
    moves.need()
    rows8 = iota((WIDTH, SIZE), 0) % 8
    gains = w_ref[:, 384:].astype(F32)
    query_gain = jnp.sum(jnp.where(rows8 == 0, gains, 0.0), 0, keepdims=True)
    key_gain = jnp.sum(jnp.where(rows8 == 1, gains, 0.0), 0, keepdims=True)
    for e in range(PLACES):
        block = proj[e]
        query, key = block[:, :128], block[:, 128:256]
        p_ref[e] = block[:, :256]
        cos, sin = cos_ref[e], sin_ref[e]
        query = query * mean_scale(query) * query_gain
        q_ref[e] = (query * cos + swap_halves(query) * sin).astype(BF16)
        key = key * mean_scale(key) * key_gain
        start = scal[2 + e]
        kc[pl.ds(start, ROWS), :] = key * cos + swap_halves(key) * sin
        vc[pl.ds(start, ROWS), :] = block[:, 256:]
    moves.flush(5)
    slots = PLACES * ROWS
    k_ref[...] = kc[:slots].astype(BF16)
    v_ref[...] = vc[:slots].astype(BF16)
    va[:, :128] = v_ref[...]
    moves.flush(1, 2, 3)

    for j in range(4):
        query = q_ref[4 * j : 4 * j + 4].reshape(512, SIZE)
        limit = row_limits(scal, 4 * j, (512, 512), 0)
        acc[...] = jnp.zeros_like(acc)

        def step(masked, query=query, limit=limit):
            def body(b, carry):
                at = pl.multiple_of(b * 512, 512)
                s = matmul_nt(query, k_ref[pl.ds(at, 512), :])
                prob = jnp.exp2(s * SCALE2)
                if masked:
                    prob = jnp.where(iota((512, 512), 1) + at <= limit, prob, 0.0)
                acc[...] += matmul(prob.astype(BF16), va[pl.ds(at, 512), :])
                return carry

            return body

        full = (scal[2 + 4 * j] + 1) // 512
        last = jnp.minimum(scal[2 + 4 * j + 3] + ROWS - 1, total - 1) // 512 + 1
        lax.fori_loop(0, full, step(False), 0)
        lax.fori_loop(full, last, step(True), 0)
        weight = acc[:, 128:]
        o_ref[4 * j : 4 * j + 4] = (
            (acc[:, :128] / weight).astype(BF16).reshape(4, ROWS, SIZE)
        )
        lse_ref[:, 512 * j : 512 * j + 512] = jnp.log2(weight).T[:8]


def attend(scal, tokens, weights, cos, sin):
    slots = PLACES * ROWS
    blocks = (PLACES, ROWS, SIZE)
    outs = [
        (blocks, BF16),
        (blocks, BF16),
        ((slots, SIZE), BF16),
        ((slots, SIZE), BF16),
        ((8, slots), F32),
        ((PLACES, ROWS, 256), F32),
        ((WIDTH, 512), BF16),
    ]
    scratch = [
        pltpu.VMEM((slots + ROWS, SIZE), F32),
        pltpu.VMEM((slots + ROWS, SIZE), F32),
        pltpu.VMEM((slots, 256), BF16),
        pltpu.VMEM((512, 256), F32),
        pltpu.VMEM((PLACES, ROWS, 384), F32),
    ]
    return call(
        attend_kernel, outs, (scal, *tokens, *weights, cos, sin), (0,), scratch=scratch,
        micros=18,
    )


def retreat_kernel(
    moves, scal, do_ref, o_ref, q_ref, k_ref, v_ref, lse_ref, w_ref, cos_ref, sin_ref, p_ref, after,
    low, gains_ref, terms_ref, dq, dk, dv, delta,
):
    total = scal[1]
    moves.need(1, 2, 3, 4, 5, 6)
    dk[...] = jnp.zeros_like(dk)
    dv[...] = jnp.zeros_like(dv)
    ones = jnp.ones((8, SIZE), F32)

    for j in range(4):
        query = q_ref[4 * j : 4 * j + 4].reshape(512, SIZE)
        grad = do_ref[4 * j : 4 * j + 4].reshape(512, SIZE)
        out = o_ref[4 * j : 4 * j + 4].reshape(512, SIZE)
        prod = grad.astype(F32) * out.astype(F32)
        delta[...] = lax.dot_general(
            ones, prod, (((1,), (1,)), ((), ())), preferred_element_type=F32,
            precision=lax.Precision.HIGHEST,
        )
        limit = row_limits(scal, 4 * j, (8, 512), 1)[:1]
        dq[j] = jnp.zeros((512, SIZE), F32)

        def step(masked, query=query, grad=grad, limit=limit, j=j):
            def body(b, carry):
                at = pl.multiple_of(b * 512, 512)
                key = k_ref[pl.ds(at, 512), :]
                s = matmul_nt(key, query)
                prob = jnp.exp2(s * SCALE2 - lse_ref[:1, 512 * j : 512 * j + 512])
                if masked:
                    prob = jnp.where(iota((512, 512), 0) + at <= limit, prob, 0.0)
                dv[pl.ds(at, 512), :] += matmul(prob.astype(BF16), grad)
                prob_grad = matmul_nt(v_ref[pl.ds(at, 512), :], grad)
                score = (prob * (prob_grad - delta[:1])).astype(BF16)
                dk[pl.ds(at, 512), :] += matmul(score, query)
                dq[j] += matmul_tn(score, key)
                return carry

            return body

        full = (scal[2 + 4 * j] + 1) // 512
        last = jnp.minimum(scal[2 + 4 * j + 3] + ROWS - 1, total - 1) // 512 + 1
        lax.fori_loop(0, full, step(False), 0)
        lax.fori_loop(full, last, step(True), 0)

    moves.need()
    rows8 = iota((WIDTH, SIZE), 0) % 8
    gains = w_ref[:, 384:].astype(F32)
    query_gain = jnp.sum(jnp.where(rows8 == 0, gains, 0.0), 0, keepdims=True)
    key_gain = jnp.sum(jnp.where(rows8 == 1, gains, 0.0), 0, keepdims=True)

    query_part = jnp.zeros((1, SIZE), F32)
    key_part = jnp.zeros((1, SIZE), F32)

    def head(grad, projected, gain, cos, sin):
        turned = grad * cos - swap_halves(grad) * sin
        scale = mean_scale(projected)
        normal = projected * scale
        part = jnp.sum(turned * normal, 0, keepdims=True)
        return norm_back(turned * gain, normal, scale).astype(BF16), part

    for e in range(PLACES):
        cos, sin = cos_ref[e], sin_ref[e]
        at = ROWS * (e % 4)
        query_grad = dq[e // 4, at : at + ROWS, :] * SCALE
        low[e, :, :128], part = head(query_grad, p_ref[e, :, :128], query_gain, cos, sin)
        query_part += part
        live = iota((ROWS, SIZE), 0) < scal[18 + e]
        start = scal[2 + e]
        key_grad = jnp.where(live, dk[pl.ds(start, ROWS), :], 0.0) * SCALE
        low[e, :, 128:256], part = head(key_grad, p_ref[e, :, 128:], key_gain, cos, sin)
        key_part += part
        low[e, :, 256:] = jnp.where(live, dv[pl.ds(start, ROWS), :], 0.0).astype(BF16)

        if e % 4 == 3:
            rows = low[e - 3 : e + 1].reshape(4 * ROWS, 384)
            terms = matmul_nt(rows, w_ref[:, :384]).astype(BF16)
            terms_ref[e - 3 : e + 1] = terms.reshape(4, ROWS, WIDTH)
    gains_ref[...] = jnp.where(iota((8, SIZE), 0) == 0, query_part, key_part)


def retreat(scal, head_grad, saved, weight, cos, sin, projected, after):
    outs = [((PLACES, ROWS, 384), BF16), ((8, SIZE), F32), ((PLACES, ROWS, WIDTH), BF16)]
    slots = PLACES * ROWS
    scratch = [
        pltpu.VMEM((4, 512, SIZE), F32),
        pltpu.VMEM((slots + ROWS, SIZE), F32),
        pltpu.VMEM((slots + ROWS, SIZE), F32),
        pltpu.VMEM((8, 512), F32),
    ]
    return call(
        retreat_kernel, outs, (scal, head_grad, *saved, weight, cos, sin, projected, after),
        (0,), (11,), scratch=scratch, micros=25,
    )


def weigh_heads_kernel(moves, scal, *refs):
    tokens, (low, gains_ref, after, mine_ref, theirs_ref, grad) = refs[:8], refs[8:]
    moves.need()
    for quarter in range(4):
        part, mode = divmod(quarter, 2)
        total = jnp.zeros((256, 384), F32)
        for half in range(2):
            blocks = [places(scal, part, SEEN[mode][2 * half + i // 4], i % 4) for i in range(8)]
            rows = jnp.concatenate([low[e] for e in blocks], 0)
            total += matmul_tn(tokens[2 * quarter + half][...].reshape(8 * ROWS, 256), rows)
        grad[256 * quarter : 256 * quarter + 256, :384] = total.astype(BF16)
    rows8 = iota((WIDTH, SIZE), 0) % 8
    spot = iota((WIDTH, SIZE), 0) // 8 == iota((WIDTH, SIZE), 1)
    extra = jnp.where(rows8 == 0, gains_ref[:1], jnp.where(rows8 == 1, gains_ref[1:2], 0.0))
    grad[:, 384:] = jnp.where(spot, extra, 0.0).astype(BF16)
    for x in range(4):
        for c, ref in enumerate((mine_ref, theirs_ref)):
            block = 2 * x + (scal[37] ^ c)
            ref[x] = grad[pl.ds(pl.multiple_of(ROWS * block, ROWS), ROWS), :]


def weigh_heads(scal, tokens, low, gains, after):
    return call(
        weigh_heads_kernel, [((4, ROWS, 512), BF16)] * 2, (scal, *tokens, low, gains, after), (0,), (11,),
        scratch=[pltpu.VMEM((WIDTH, 512), BF16)], micros=7,
    )


def feed_kernel(
    moves, scal, mixed_ref, x_ref, cot_ref, ff_ref,
    out_ref, mg_ref, send_ref, mine_ref, theirs_ref, right_ref,
    w, sems, gate, up, half, normal,
):
    core, count = scal[0], scal[1]
    copies = [pltpu.make_async_copy(ff_ref.at[u], w.at[u], sems.at[u]) for u in range(UNITS)]
    for u in (0, 1, 2, 5, 8, 3, 6, 9, 4, 7, 10):
        copies[u].start()

    def left(unit, value):
        even = jnp.concatenate([value[:, 256 * i : 256 * i + 128] for i in range(4)], 1)
        odd = jnp.concatenate([value[:, 256 * i + 128 : 256 * i + 256] for i in range(4)], 1)
        at = slice(512 * unit, 512 * unit + 512)
        mine_ref[:, at] = jnp.where(core == 0, even, odd)
        theirs_ref[:, at] = jnp.where(core == 0, odd, even)

    low_lanes = iota((ROWS, SIZE), 1) < 64
    moves.need()
    for i in range(8):
        a, b = mixed_ref[2 * i].astype(F32), mixed_ref[2 * i + 1].astype(F32)
        at = slice(128 * i, 128 * i + 128)
        half[0, :, at] = jnp.where(low_lanes, a, swap_halves(b)).astype(BF16)
        half[1, :, at] = jnp.where(low_lanes, swap_halves(a), b).astype(BF16)
    out_ref[...] = x_ref[...]
    for t in range(2):
        left(t, half[t])
        copies[t].wait()
        out_ref[...] += matmul(half[t], w[t])
    middle = out_ref[...]
    scale = mean_scale(middle)
    normal[...] = middle * scale
    normal_low = normal[...].astype(BF16)
    left(2, normal_low)
    live = iota((ROWS, 1), 0) < count
    branch = jnp.where(live, cot_ref[...], 0.0).astype(BF16)
    right_ref[:, 7 * WIDTH :] = branch
    mg_ref[...] = jnp.zeros_like(mg_ref)
    for t in range(3):
        copies[2 + t].wait()
        copies[5 + t].wait()
        copies[8 + t].wait()
        gate[...] = matmul(normal_low, w[2 + t])
        up[...] = matmul(normal_low, w[5 + t])
        g, u = gate[...], up[...]
        sig = 0.5 + 0.5 * jnp.tanh(0.5 * g)
        inner = (g * sig * u).astype(BF16)
        left(3 + t, inner)
        out_ref[...] += matmul(inner, w[8 + t])
        grad_inner = matmul_nt(branch, w[8 + t])
        gate_grad = (grad_inner * u * sig * (1.0 + g * (1.0 - sig))).astype(BF16)
        up_grad = (grad_inner * g * sig).astype(BF16)
        right_ref[:, WIDTH * (1 + t) : WIDTH * (2 + t)] = gate_grad
        right_ref[:, WIDTH * (4 + t) : WIDTH * (5 + t)] = up_grad
        mg_ref[...] += matmul_nt(gate_grad, w[2 + t])
        mg_ref[...] += matmul_nt(up_grad, w[5 + t])
    moves.flush(0, 3, 4)
    middle_grad = jnp.where(live, cot_ref[...], 0.0) + norm_back(mg_ref[...], normal[...], scale)
    mg_ref[...] = middle_grad
    attn_grad = middle_grad.astype(BF16)
    right_ref[:, :WIDTH] = attn_grad
    moves.flush(1, 5)
    first = matmul_nt(attn_grad, w[0])
    second = matmul_nt(attn_grad, w[1])
    for i in range(8):
        a, b = first[:, 128 * i : 128 * i + 128], second[:, 128 * i : 128 * i + 128]
        send_ref[2 * i] = jnp.where(low_lanes, a, swap_halves(b)).astype(BF16)
        send_ref[2 * i + 1] = jnp.where(low_lanes, swap_halves(a), b).astype(BF16)


def feed(scal, mixed, x, cotangent, ff):
    outs = [
        ((ROWS, WIDTH), F32),
        ((ROWS, WIDTH), F32),
        ((HEADS, ROWS, SIZE), BF16),
        ((ROWS, 3072), BF16),
        ((ROWS, 3072), BF16),
        ((ROWS, 8 * WIDTH), BF16),
    ]
    scratch = [
        pltpu.VMEM((UNITS, WIDTH, WIDTH), BF16),
        pltpu.SemaphoreType.DMA((UNITS,)),
        pltpu.VMEM((ROWS, WIDTH), F32),
        pltpu.VMEM((ROWS, WIDTH), F32),
        pltpu.VMEM((2, ROWS, WIDTH), BF16),
        pltpu.VMEM((ROWS, WIDTH), F32),
    ]
    return call(
        feed_kernel, outs, (scal, mixed, x, cotangent, ff), (0,), (4,), scratch=scratch,
        micros=22,
    )


def weigh_kernel(moves, scal, lm_ref, lt_ref, rm_ref, rt_ref, *refs):
    outs, (left, right), buffers = refs[:10], refs[10:12], refs[12:]
    moves.need(1, 2)
    for l in range(6):
        at = slice(512 * l, 512 * l + 512)
        left[at, :128] = lm_ref[:, at].astype(F32).T.astype(BF16)
        left[at, 128:] = lt_ref[:, at].astype(F32).T.astype(BF16)
    moves.need()
    right[:128] = rm_ref[...]
    right[128:] = rt_ref[...]
    for s, (part, mode, halves) in enumerate(QUARTERS):
        buffer = buffers[s]
        for n, (unit, c) in enumerate(halves):
            l, r = PAIRS[unit]
            at = WIDTH * r + 512 * c
            out = matmul(left[512 * l : 512 * l + 512], right[:, at : at + 512])
            for i in range(4):
                if part == 0:
                    block = out[128 * i : 128 * i + 128]
                elif part == 1:
                    rows = [128 * x + 32 * i for x in range(4)]
                    block = jnp.concatenate([out[r : r + 32] for r in rows], 0)
                else:
                    rows = [32 * j + 8 * i for j in range(16)]
                    block = jnp.concatenate([out[r : r + 8] for r in rows], 0)
                buffer[i, n] = block.astype(BF16)
        for i, mask in enumerate(KEPT[mode]):
            moves.push(buffer.at[scal[part] ^ mask], outs[2 * s + i // 2].at[i % 2])


def weigh(scal, mine, theirs, right, right_theirs):
    outs = [((2, len(h), 128, 512), BF16) for p, m, h in QUARTERS for i in range(2)]
    scratch = [pltpu.VMEM((3072, 256), BF16), pltpu.VMEM((256, 8 * WIDTH), BF16)]
    scratch += [pltpu.VMEM((4, len(h), 128, 512), BF16) for p, m, h in QUARTERS]
    out = call(
        weigh_kernel, outs, (scal, mine, theirs, right, right_theirs), (0,), (), range(10),
        scratch, micros=9, sends=20,
    )
    return out[::2], out[1::2]


AXES = ("x", "y", "z")


def add(a, b):
    return a.astype(F32) + b.astype(F32)


def four(refs):
    return add(refs[0][...], refs[1][...]) + add(refs[2][...], refs[3][...])


def add_first_kernel(moves, *refs):
    keeps, gots, (after,), refs = refs[:5], refs[5:10], refs[10:11], refs[11:]
    new_keeps, new_sends = refs[:5], refs[5:]
    for s in range(5):
        moves.need(s, 5 + s)
        new_sends[s][...] = add(keeps[s][1], gots[s][1]).astype(BF16)
        moves.flush(5 + s)
    for s in range(5):
        new_keeps[s][...] = add(keeps[s][0], gots[s][0]).astype(BF16)
        moves.flush(s)


def add_first(keeps, gots, after):
    outs = [(k.shape[1:], BF16) for k in keeps] * 2
    order = [i for s in range(5) for i in (s, 5 + s)]
    out = call(
        add_first_kernel, outs, (*keeps, *gots, after), anywhere=(10,), micros=6, order=order
    )
    return out[:5], out[5:]


PART_ROWS = 32 * len(PARTS[0])
MORE_ROWS = 32 * len(PARTS[2])


SEQUENCE = (2, 3, 0, 1, 4)


def join_kernel(moves, scal, *refs):
    keeps, gots, outs, buffers = refs[:5], refs[5:10], refs[10:18], refs[18:]
    for s in SEQUENCE:
        part, mode, halves = QUARTERS[s]
        moves.need(1 + s, 6 + s)
        first = 32 * 5 * mode
        for n in range(len(halves)):
            total = add(keeps[s][n], gots[s][n])
            at = first + 32 * n
            for i in range(4):
                if part < 2:
                    buffers[part][i, at : at + 32] = total[32 * i : 32 * i + 32].astype(BF16)
                else:
                    rows = [total[32 * x + 8 * i : 32 * x + 8 * i + 8] for x in range(4)]
                    at = PART_ROWS + 32 * n
                    buffers[0][i, at : at + 32] = jnp.concatenate(rows, 0).astype(BF16)
        if s == 3:
            for mask in range(4):
                moves.push(buffers[1].at[scal[0] ^ mask], outs[4 + mask])
    for mask in range(4):
        moves.push(buffers[0].at[scal[1] ^ mask], outs[mask])


def join(scal, keeps, gots):
    shapes = [(PART_ROWS + MORE_ROWS, 512), (PART_ROWS, 512)]
    outs = [(shape, BF16) for shape in shapes for mask in range(4)]
    order = [i for s in SEQUENCE for i in (1 + s, 6 + s)]
    return call(
        join_kernel, outs, (scal, *keeps, *gots), (0,), (), range(8),
        [pltpu.VMEM((4, *shape), BF16) for shape in shapes], micros=5, sends=8, order=order,
    )


def add_heads_kernel(moves, scal, mine_ref, theirs_ref, *refs):
    outs, buffer = refs[:4], refs[4]
    moves.need()
    for x in range(4):
        buffer[x] = add(mine_ref[x], theirs_ref[x]).astype(BF16)
    for mask in range(4):
        moves.push(buffer.at[scal[0] ^ mask], outs[mask])


def add_heads(scal, mine, theirs):
    return call(
        add_heads_kernel, [((ROWS, 512), BF16)] * 4, (scal, mine, theirs), (0,), raw=range(4),
        scratch=[pltpu.VMEM((4, ROWS, 512), BF16)], limit=12, micros=2, sends=4,
    )


def sum_heads_kernel(moves, *refs):
    moves.need()
    total = four(refs[:4])
    for f in range(HEADS):
        refs[4][f] = total[8 * f : 8 * f + 8].astype(BF16)


def sum_heads(got):
    return call(sum_heads_kernel, [((HEADS, 8, 512), BF16)], tuple(got), limit=12, micros=2)[0]


def pass_on_kernel(moves, scal, *refs):
    got, outs, buffer, small = refs[:8], refs[8:16], refs[16], refs[17]
    for part in (1, 0):
        moves.need(*range(1 + 4 * part, 5 + 4 * part))
        total = four(got[4 * part : 4 * part + 4])
        for n in range(len(PARTS[part])):
            for i in range(4):
                at = PART_ROWS // 4 * part + 8 * n
                buffer[i, at : at + 8] = total[32 * n + 8 * i : 32 * n + 8 * i + 8].astype(BF16)
    for mask in range(4):
        moves.push(buffer.at[scal[2] ^ mask], outs[mask])
    for n in range(len(PARTS[2])):
        for i in range(4):
            at = PART_ROWS + 32 * n + 8 * i
            small[i, 8 * n : 8 * n + 8] = total[at : at + 8].astype(BF16)
    for mask in range(4):
        moves.push(small.at[scal[0] ^ mask], outs[4 + mask])


def pass_on(scal, got):
    shapes = [(PART_ROWS // 2, 512), (MORE_ROWS // 4, 512)]
    outs = [(shape, BF16) for shape in shapes for mask in range(4)]
    return call(
        pass_on_kernel, outs, (scal, *got), (0,), raw=range(8), limit=12, still=(2, 3, 4, 6, 7, 8),
        scratch=[pltpu.VMEM((4, *shape), BF16) for shape in shapes], micros=4, sends=8,
    )


def finish_heads_kernel(
    moves, back_ref, q_ref, k_ref, v_ref, g1_ref, dq_ref, dk_ref, dv_ref, dg_ref, dqk_ref
):
    moves.need()
    gain = column(g1_ref[...].astype(BF16).astype(F32))
    order = channel_map(True)
    dg = jnp.zeros((8, 1), F32)
    extra = jnp.zeros((8, SIZE), F32)
    for h in range(KV_HEADS):
        pair = []
        for f in (2 * h, 2 * h + 1):
            total = back_ref[f].astype(F32)
            at = slice(128 * f, 128 * f + 128)
            dq_ref[0, :, at] = total[:, :128] * gain
            w = q_ref[0, :, at].astype(BF16).astype(F32)
            dg += jnp.sum(total[:, :128] * w, 1, keepdims=True)
            extra += total[:, 384:]
            pair.append(total)
        at = slice(128 * h, 128 * h + 128)
        both = pair[0] + pair[1]
        dk = both[:, 128:256]
        dv = exact(both[:, 256:384], order)
        dk_ref[0, :, at] = dk * gain
        dv_ref[0, :, at] = dv * gain
        dg += jnp.sum(dk * k_ref[0, :, at].astype(BF16).astype(F32), 1, keepdims=True)
        dg += jnp.sum(dv * v_ref[0, :, at].astype(BF16).astype(F32), 1, keepdims=True)
    dg_ref[...] = jnp.sum(jnp.where(iota((8, 8), 0) == iota((8, 8), 1), dg, 0.0), 0, keepdims=True)
    dqk_ref[...] = jnp.broadcast_to(jnp.sum(extra, 1, keepdims=True), (8, SIZE))


def finish_heads(back, q, k, v, g1):
    outs = [((1, 8, 2048), F32), ((1, 8, 1024), F32), ((1, 8, 1024), F32), ((1, 8), F32), ((8, SIZE), F32)]
    return call(finish_heads_kernel, outs, (back, q, k, v, g1), micros=2)


def finish_feed_kernel(moves, *refs):
    got, more, (g_ref, u_ref, g2_ref), outs = refs[:4], refs[4:8], refs[8:11], refs[13:]
    do_ref, dg_ref, du_ref, dd_ref, gain_ref = outs
    moves.need()
    total = jnp.concatenate([four(got), four(more)], 0)
    tiles = {key: total[8 * n : 8 * n + 8] for n, key in enumerate(HALVES)}
    units = [jnp.concatenate([tiles[u, 0], tiles[u, 1]], 1) for u in range(UNITS)]
    for t in range(2):
        do_ref[0, 8 * t : 8 * t + 8] = units[t]
    for t in range(3):
        dd_ref[0, 8 * t : 8 * t + 8] = units[8 + t]
    gain = column(g2_ref[...].astype(BF16).astype(F32))
    order = hidden_map(True)
    dg = jnp.zeros((8, 1), F32)
    for base, w_ref, out_ref in ((2, g_ref, dg_ref), (5, u_ref, du_ref)):
        tall = jnp.concatenate(
            [
                jnp.concatenate([units[base + t][:, 128 * i : 128 * i + 128] for t in range(3)], 1)
                for i in range(8)
            ],
            0,
        )
        tall = exact(tall, order)
        for i in range(8):
            at = slice(384 * i, 384 * i + 384)
            grad = tall[8 * i : 8 * i + 8]
            dg += jnp.sum(grad * w_ref[0, :, at].astype(BF16).astype(F32), 1, keepdims=True)
            out_ref[0, :, at] = grad * gain
    gain_ref[...] = jnp.sum(jnp.where(iota((8, 8), 0) == iota((8, 8), 1), dg, 0.0), 0, keepdims=True)


def finish_feed(got, gate, up, g2, *after):
    outs = [
        ((1, 16, 1024), F32), ((1, 8, 3072), F32), ((1, 8, 3072), F32), ((1, 24, 1024), F32), ((1, 8), F32),
    ]
    return call(
        finish_feed_kernel, outs, (*got, gate, up, g2, *after), anywhere=(11, 12), limit=12, micros=3,
        still=range(8),
    )


def finish_input_kernel(moves, part_ref, x_ref, mg_ref, out_ref):
    moves.need()
    x = x_ref[...]
    scale = mean_scale(x)
    out_ref[...] = mg_ref[...] + norm_back(part_ref[...].astype(F32), x * scale, scale)


def finish_input(part, x, middle_grad):
    return call(finish_input_kernel, [((ROWS, WIDTH), F32)], (part, x, middle_grad), micros=2)[0]


def other(v):
    return lax.ppermute(v, "core", [(0, 1), (1, 0)])


def trade(v, axes):
    return lax.all_to_all(v, axes, split_axis=0, concat_axis=0, tiled=True)


def exchange(v, axis, mask):
    return lax.ppermute(v, axis, [(i, i ^ mask) for i in range(4)])


def swap(terms, axis):
    return [terms[0]] + [exchange(terms[mask], axis, mask) for mask in (1, 3, 2)]


def in_order(v):
    return [v[0], v[1], v[3], v[2]]


def shards(
    block_input, counts, query_weight, key_matrix, value_matrix, out_weight, gate_weight,
    up_weight, down_weight, attn_gain, mlp_gain, query_gain, key_gain, cotangent,
):
    place = lax.axis_index(TOKENS)
    group = lax.axis_index(("x", "core"))
    core = lax.axis_index("core")
    own = lax.axis_index(ALL).reshape(1).astype(jnp.int32)
    ff_pack = pack_feed(out_weight, gate_weight, up_weight, down_weight, mlp_gain)
    ff = lax.all_gather(ff_pack, ALL, axis=1, tiled=True)
    early, late = prepare(block_input, ff_pack)
    blocks = [swap([early] * 4, "y"), swap([late] * 4, "z")]
    head_send = pack_heads(
        own, query_gain, key_gain, query_weight, key_matrix, value_matrix, attn_gain, ff_pack
    )
    head_weights = jnp.stack(in_order(swap([trade(head_send, TOKENS).reshape(ROWS, 512)] * 4, "x")))
    head_weights = (head_weights, other(head_weights))
    tokens = []
    for block, axis in zip(blocks, "zy"):
        block = jnp.stack(in_order(block))
        for mode in range(2):
            piece = block[:, :, 256 * mode : 256 * mode + 256]
            both = jnp.stack([piece, exchange(piece, axis, MASKS[mode][0])])
            tokens += [both, exchange(both, axis, MASKS[mode][1])]

    group_counts = lax.dynamic_index_in_dim(counts, group, 0, keepdims=False)
    starts = jnp.cumsum(group_counts) - group_counts
    own_count = lax.dynamic_index_in_dim(group_counts, place, 0, keepdims=False)
    scal = jnp.concatenate(
        [place.reshape(1), jnp.sum(group_counts).reshape(1), starts, group_counts]
        + [lax.axis_index(a).reshape(1) for a in ("y", "z", "x", "core")]
    ).astype(jnp.int32)
    inverse = ROPE_BASE ** (-(jnp.arange(64, dtype=F32) * 2.0 / SIZE))
    position = starts[:, None] + jnp.arange(ROWS, dtype=jnp.int32)[None, :]
    angles = position.astype(F32)[:, :, None] * inverse
    cosine, sine = jnp.cos(angles), jnp.sin(angles)
    cos = jnp.concatenate([cosine, cosine], -1)
    sin = jnp.concatenate([-sine, sine], -1)

    mixed_head, *saved, projected, head_weight = attend(scal, tokens, head_weights, cos, sin)
    mixed = trade(mixed_head, TOKENS)
    block_output, middle_grad, grad_send, mine, theirs, right = feed(
        jnp.stack([core, own_count]).astype(jnp.int32), mixed, block_input, cotangent, ff
    )
    head_grad = trade(grad_send, TOKENS)

    chip = jnp.stack([lax.axis_index(a) for a in AXES]).astype(jnp.int32)
    keeps, sends = weigh(chip, mine, other(theirs), right, other(right))
    sends, head_grad = lax.optimization_barrier((sends, head_grad))

    def step(sends, order):
        return [
            exchange(v, FIRST[part], MASKS[mode][order])
            for v, (part, mode, halves) in zip(sends, QUARTERS)
        ]

    gots = step(sends, 0)
    low, head_gains, token_terms = retreat(
        scal, head_grad, [mixed_head] + saved, head_weight, cos, sin, projected, sends[0]
    )
    gots, token_terms = lax.optimization_barrier((gots, token_terms))
    token_sum = lax.psum_scatter(
        token_terms.reshape(PLACES * ROWS, WIDTH), TOKENS, scatter_dimension=0, tiled=True
    )
    keeps, sends = add_first(keeps, gots, head_gains)
    gots = step(sends, 1)
    head_mine, head_theirs = weigh_heads(scal, tokens, low, head_gains, sends[0])
    heads = swap(add_heads(chip, head_mine, other(head_theirs)), "x")
    head_back = trade(sum_heads(heads), TOKENS)
    terms = join(chip, keeps, gots)
    terms = pass_on(chip, swap(terms[:4], "y") + swap(terms[4:], "x"))
    got = swap(terms[:4], "z") + swap(terms[4:], "x")
    input_grad = finish_input(token_sum, block_input, middle_grad)
    query_grad, key_grad, value_grad, attn_gain_grad, head_gains = finish_heads(
        head_back, query_weight, key_matrix, value_matrix, attn_gain
    )
    out_grad, gate_grad, up_grad, down_grad, mlp_gain_grad = finish_feed(
        got, gate_weight, up_weight, mlp_gain, input_grad, head_gains
    )
    return (
        block_output,
        input_grad,
        query_grad,
        key_grad,
        value_grad,
        out_grad,
        gate_grad,
        up_grad,
        down_grad,
        attn_gain_grad,
        mlp_gain_grad,
        head_gains[0:1, 0:1],
        head_gains[1:2, 0:1],
    )


def solution(mesh):
    fine = Mesh(mesh.devices.reshape(4, 2, 4, 4), ALL)
    tokens = P(ALL, None)
    weight = P(None, ALL, None)
    gain = P(None, ALL)
    return jax.shard_map(
        shards,
        mesh=fine,
        in_specs=(tokens, P()) + (weight,) * 7 + (gain,) * 4 + (tokens,),
        out_specs=(tokens, tokens) + (weight,) * 7 + (gain,) * 4,
        check_vma=False,
    )
```

```python
import functools

import jax
import jax.numpy as jnp
from jax import lax
from jax.experimental import pallas as pl
from jax.experimental.pallas import tpu as pltpu
from jax.sharding import Mesh, PartitionSpec as P

HEADS = 16
KV_HEADS = 8
SIZE = 128
WIDTH = 1024
ROWS = 128
PLACES = 16
EPSILON = 1e-06
ROPE_BASE = 1000000.0
SCALE = SIZE**-0.5
SCALE2 = SCALE * 1.4426950408889634
F32 = jnp.float32
BF16 = jnp.bfloat16
MIB = 1 << 20
US = 3_600_000

TOKENS = ("y", "z")
ALL = ("x", "core", "y", "z")

UNITS = 11
COLUMNS = 256
PIECES = [(u, c) for u in range(UNITS) for c in range(4)]
PARTS = [PIECES[:18], PIECES[18:36], PIECES[36:]]
FIRST = ("x", "y", "z")
MASKS = ((1, 3), (3, 1))
KEPT = ((0, 3, 1, 2), (0, 1, 3, 2))
SEEN = ((0, 1, 3, 2), (0, 3, 1, 2))
SHARES = [
    (0, 0, PARTS[0][:9]), (0, 1, PARTS[0][9:]), (1, 0, PARTS[1][:9]), (1, 1, PARTS[1][9:]), (2, 0, PARTS[2]),
]
PAIRS = [(0, 0), (1, 0)] + [(2, 1 + t) for t in range(6)] + [(3 + t, 7) for t in range(3)]


def matmul(a, b):
    return lax.dot_general(a, b, (((1,), (0,)), ((), ())), preferred_element_type=F32)


def matmul_nt(a, b):
    return lax.dot_general(a, b, (((1,), (1,)), ((), ())), preferred_element_type=F32)


def matmul_tn(a, b):
    return lax.dot_general(a, b, (((0,), (0,)), ((), ())), preferred_element_type=F32)


def exact(a, b):
    return lax.dot_general(
        a, b, (((1,), (0,)), ((), ())), preferred_element_type=F32, precision=lax.Precision.HIGHEST
    )


SMEM = pl.BlockSpec(memory_space=pltpu.SMEM)
HBM = pl.BlockSpec(memory_space=pltpu.HBM)
VMEM = pl.BlockSpec(memory_space=pltpu.VMEM)


class Moves:
    def __init__(self, ins, outs, sems):
        self.ins, self.outs, self.sems, self.sent, self.pushed = ins, outs, sems, [], 0

    def need(self, *which):
        for i in which or list(self.ins):
            if i in self.ins:
                self.ins.pop(i).wait()

    def flush(self, *which):
        for i in which or list(self.outs):
            if i in self.outs:
                copy = self.outs.pop(i)
                copy.start()
                self.sent.append(copy)

    def push(self, source, target):
        copy = pltpu.make_async_copy(source, target, self.sems.at[self.pushed])
        copy.start()
        self.sent.append(copy)
        self.pushed += 1

    def finish(self):
        self.need()
        self.flush()
        for copy in self.sent:
            copy.wait()


def call(
    kernel, outs, args, scalars=(), anywhere=(), raw=(), scratch=(), limit=60, micros=1, sends=0, order=None, still=()
):
    moved = [i for i in range(len(args)) if i not in (*scalars, *anywhere, *still)]
    made = [i for i in range(len(outs)) if i not in raw]
    count, total = len(args), len(outs)

    def body(*refs):
        ins, out, rest = list(refs[:count]), list(refs[count : count + total]), list(refs[count + total :])
        here = [rest.pop(0) for i in moved]
        there = [rest.pop(0) for i in made]
        sems_in, sems_out = rest.pop(0), rest.pop(0)
        copies_in = {i: pltpu.make_async_copy(ins[i], here[n], sems_in.at[n]) for n, i in enumerate(moved)}
        copies_out = {
            i: pltpu.make_async_copy(there[n], out[i], sems_out.at[sends + n]) for n, i in enumerate(made)
        }
        for i in order or moved:
            copies_in[i].start()
        for n, i in enumerate(moved):
            ins[i] = here[n]
        for n, i in enumerate(made):
            out[i] = there[n]
        moves = Moves(copies_in, copies_out, sems_out)
        kernel(moves, *ins, *out, *rest)
        moves.finish()

    buffers = [pltpu.VMEM(args[i].shape, args[i].dtype) for i in moved]
    buffers += [pltpu.VMEM(*outs[i]) for i in made]
    sems = [pltpu.SemaphoreType.DMA((max(len(moved), 1),)), pltpu.SemaphoreType.DMA((len(made) + sends,))]
    return pl.pallas_call(
        body,
        out_shape=[jax.ShapeDtypeStruct(s, t) for s, t in outs],
        in_specs=[SMEM if i in scalars else VMEM if i in still else HBM for i in range(count)],
        out_specs=[HBM] * total,
        scratch_shapes=buffers + sems + list(scratch),
        compiler_params=pltpu.CompilerParams(vmem_limit_bytes=limit * MIB),
        cost_estimate=pl.CostEstimate(flops=0, bytes_accessed=US * micros, transcendentals=0),
    )(*args)


def iota(shape, dim):
    return lax.broadcasted_iota(jnp.int32, shape, dim)


def mean_scale(v):
    return lax.rsqrt(jnp.mean(v * v, -1, keepdims=True) + EPSILON)


def norm_back(grad, normal, scale):
    return scale * (grad - normal * jnp.mean(grad * normal, -1, keepdims=True))


def swap_halves(v):
    return pltpu.roll(v, 64, 1)


def column(row):
    return jnp.sum(jnp.where(iota((8, 8), 0) == iota((8, 8), 1), row, 0.0), 1, keepdims=True)


def hidden_map(back):
    shape = (384, 384)
    source, target = (iota(shape, 1), iota(shape, 0)) if back else (iota(shape, 0), iota(shape, 1))
    i, rest = source // 24, source % 24
    return jnp.where((rest // 8) * 128 + i * 8 + rest % 8 == target, 1.0, 0.0)


def channel_map(back):
    shape = (128, 128)
    source, target = (iota(shape, 1), iota(shape, 0)) if back else (iota(shape, 0), iota(shape, 1))
    i, rest = source // 16, source % 16
    return jnp.where((rest // 8) * 64 + i * 8 + rest % 8 == target, 1.0, 0.0)


def pack_feed_kernel(moves, o_ref, g_ref, u_ref, d_ref, g2_ref, ff_ref):
    moves.need()
    gain2 = column(g2_ref[...].astype(BF16).astype(F32))
    for t in range(2):
        ff_ref[t] = o_ref[0, 8 * t : 8 * t + 8].astype(BF16)
    for t in range(3):
        ff_ref[8 + t] = d_ref[0, 8 * t : 8 * t + 8].astype(BF16)
    order = hidden_map(False).astype(BF16)
    for base, ref in ((2, g_ref), (5, u_ref)):
        w = (ref[0].astype(BF16).astype(F32) * gain2).astype(BF16).astype(F32)
        tall = jnp.concatenate([w[:, 384 * i : 384 * i + 384] for i in range(8)], 0).astype(BF16)
        tall = matmul(tall, order)
        for t in range(3):
            for i in range(8):
                ff_ref[base + t, :, 128 * i : 128 * i + 128] = tall[
                    8 * i : 8 * i + 8, 128 * t : 128 * t + 128
                ].astype(BF16)


def pack_feed(out_weight, gate, up, down, gain2):
    outs = [((UNITS, 8, WIDTH), BF16)]
    return call(pack_feed_kernel, outs, (out_weight, gate, up, down, gain2), micros=2)[0]


def prepare_kernel(moves, x_ref, after, n0_ref, n1_ref):
    moves.need()
    x = x_ref[...]
    normal = (x * mean_scale(x)).astype(BF16)
    n0_ref[...] = normal[:, :512]
    n1_ref[...] = normal[:, 512:]


def prepare(x, after):
    return call(prepare_kernel, [((ROWS, 512), BF16)] * 2, (x, after), anywhere=(1,), micros=1)


def pack_heads_kernel(moves, own, gq_ref, gk_ref, q_ref, k_ref, v_ref, g1_ref, after, send_ref):
    moves.need()
    gain1 = column(g1_ref[...].astype(BF16).astype(F32))

    def scaled(ref):
        return (ref[0].astype(BF16).astype(F32) * gain1).astype(BF16)

    query = scaled(q_ref)
    key = scaled(k_ref)
    value = scaled(v_ref).astype(F32)
    value = jnp.concatenate([value[:, 128 * i : 128 * i + 128] for i in range(8)], 0).astype(BF16)
    value = matmul(value, channel_map(False).astype(BF16))
    spot = iota((8, SIZE), 1) == own[0]
    row = iota((8, SIZE), 0)
    gq = jnp.full((8, SIZE), gq_ref[0, 0], F32).astype(BF16).astype(F32)
    gk = jnp.full((8, SIZE), gk_ref[0, 0], F32).astype(BF16).astype(F32)
    gains = jnp.where(spot & (row == 0), gq, jnp.where(spot & (row == 1), gk, 0.0)).astype(BF16)
    for f in range(HEADS):
        h = f // 2
        tile = jnp.concatenate(
            [
                query[:, 128 * f : 128 * f + 128],
                key[:, 128 * h : 128 * h + 128],
                value[8 * h : 8 * h + 8].astype(BF16),
                gains,
            ],
            1,
        )
        send_ref[f] = tile


def pack_heads(own, gq, gk, q, k, v, g1, after):
    return call(
        pack_heads_kernel, [((HEADS, 8, 512), BF16)], (own, gq, gk, q, k, v, g1, after),
        scalars=(0, 1, 2), anywhere=(7,), micros=2,
    )[0]


def row_limits(scal, first, shape, along):
    at = iota(shape, along)
    block, offset = at // ROWS, at % ROWS
    start = jnp.zeros(shape, jnp.int32)
    for i in range(4):
        start = jnp.where(block == i, scal[2 + first + i], start)
    return jnp.minimum(start + offset, scal[1] - 1)


def places(scal, part, late, early):
    first, second = scal[34 + part] ^ early, scal[35 - part] ^ late
    return 4 * first + second if part == 0 else 4 * second + first


def attend_kernel(moves, scal, *refs):
    tokens, (own_ref, other_ref, cos_ref, sin_ref) = refs[:8], refs[8:12]
    o_ref, q_ref, k_ref, v_ref, lse_ref, p_ref, w_ref, kc, vc, va, acc, proj = refs[12:]
    total = scal[1]
    kc[...] = jnp.zeros_like(kc)
    vc[...] = jnp.zeros_like(vc)
    va[:, 128:] = jnp.ones((PLACES * ROWS, 128), BF16)
    moves.need(9, 10)
    for mask in range(4):
        for c, ref in enumerate((own_ref, other_ref)):
            block = 2 * (scal[36] ^ mask) + (scal[37] ^ c)
            w_ref[pl.ds(pl.multiple_of(ROWS * block, ROWS), ROWS), :] = ref[mask]
    moves.flush(6)
    for quarter in range(4):
        part, mode = divmod(quarter, 2)
        w = w_ref[256 * quarter : 256 * quarter + 256, :384]
        for half in range(2):
            moves.need(1 + 2 * quarter + half)
            rows = tokens[2 * quarter + half][...].reshape(8 * ROWS, 256)
            out = matmul(rows, w)
            for i in range(8):
                e = places(scal, part, SEEN[mode][2 * half + i // 4], i % 4)
                block = out[ROWS * i : ROWS * i + ROWS]
                if quarter == 0:
                    proj[e] = block
                else:
                    proj[e] += block
    moves.need()
    rows8 = iota((WIDTH, SIZE), 0) % 8
    gains = w_ref[:, 384:].astype(F32)
    query_gain = jnp.sum(jnp.where(rows8 == 0, gains, 0.0), 0, keepdims=True)
    key_gain = jnp.sum(jnp.where(rows8 == 1, gains, 0.0), 0, keepdims=True)
    for e in range(PLACES):
        block = proj[e]
        query, key = block[:, :128], block[:, 128:256]
        p_ref[e] = block[:, :256]
        cos, sin = cos_ref[e], sin_ref[e]
        query = query * mean_scale(query) * query_gain
        q_ref[e] = (query * cos + swap_halves(query) * sin).astype(BF16)
        key = key * mean_scale(key) * key_gain
        start = scal[2 + e]
        kc[pl.ds(start, ROWS), :] = key * cos + swap_halves(key) * sin
        vc[pl.ds(start, ROWS), :] = block[:, 256:]
    moves.flush(5)
    slots = PLACES * ROWS
    k_ref[...] = kc[:slots].astype(BF16)
    v_ref[...] = vc[:slots].astype(BF16)
    va[:, :128] = v_ref[...]
    moves.flush(1, 2, 3)

    for j in range(4):
        query = q_ref[4 * j : 4 * j + 4].reshape(512, SIZE)
        limit = row_limits(scal, 4 * j, (512, 512), 0)
        acc[...] = jnp.zeros_like(acc)

        def step(masked, query=query, limit=limit):
            def body(b, carry):
                at = pl.multiple_of(b * 512, 512)
                s = matmul_nt(query, k_ref[pl.ds(at, 512), :])
                prob = jnp.exp2(s * SCALE2)
                if masked:
                    prob = jnp.where(iota((512, 512), 1) + at <= limit, prob, 0.0)
                acc[...] += matmul(prob.astype(BF16), va[pl.ds(at, 512), :])
                return carry

            return body

        full = (scal[2 + 4 * j] + 1) // 512
        last = jnp.minimum(scal[2 + 4 * j + 3] + ROWS - 1, total - 1) // 512 + 1
        lax.fori_loop(0, full, step(False), 0)
        lax.fori_loop(full, last, step(True), 0)
        weight = acc[:, 128:]
        o_ref[4 * j : 4 * j + 4] = (
            (acc[:, :128] / weight).astype(BF16).reshape(4, ROWS, SIZE)
        )
        lse_ref[:, 512 * j : 512 * j + 512] = jnp.log2(weight).T[:8]


def attend(scal, tokens, weights, cos, sin):
    slots = PLACES * ROWS
    blocks = (PLACES, ROWS, SIZE)
    outs = [
        (blocks, BF16),
        (blocks, BF16),
        ((slots, SIZE), BF16),
        ((slots, SIZE), BF16),
        ((8, slots), F32),
        ((PLACES, ROWS, 256), F32),
        ((WIDTH, 512), BF16),
    ]
    scratch = [
        pltpu.VMEM((slots + ROWS, SIZE), F32),
        pltpu.VMEM((slots + ROWS, SIZE), F32),
        pltpu.VMEM((slots, 256), BF16),
        pltpu.VMEM((512, 256), F32),
        pltpu.VMEM((PLACES, ROWS, 384), F32),
    ]
    return call(
        attend_kernel, outs, (scal, *tokens, *weights, cos, sin), (0,), scratch=scratch,
        micros=18,
    )


def retreat_kernel(
    moves, scal, do_ref, o_ref, q_ref, k_ref, v_ref, lse_ref, w_ref, cos_ref, sin_ref, p_ref, after,
    low, gains_ref, terms_ref, dq, dk, dv, delta, terms_vmem,
):
    total = scal[1]
    moves.need(1, 2, 3, 4, 5, 6)
    dk[...] = jnp.zeros_like(dk)
    dv[...] = jnp.zeros_like(dv)
    ones = jnp.ones((8, SIZE), F32)

    for j in range(4):
        query = q_ref[4 * j : 4 * j + 4].reshape(512, SIZE)
        grad = do_ref[4 * j : 4 * j + 4].reshape(512, SIZE)
        out = o_ref[4 * j : 4 * j + 4].reshape(512, SIZE)
        prod = grad.astype(F32) * out.astype(F32)
        delta[...] = lax.dot_general(
            ones, prod, (((1,), (1,)), ((), ())), preferred_element_type=F32,
            precision=lax.Precision.HIGHEST,
        )
        limit = row_limits(scal, 4 * j, (8, 512), 1)[:1]
        dq[j] = jnp.zeros((512, SIZE), F32)

        def step(masked, query=query, grad=grad, limit=limit, j=j):
            def body(b, carry):
                at = pl.multiple_of(b * 512, 512)
                key = k_ref[pl.ds(at, 512), :]
                s = matmul_nt(key, query)
                prob = jnp.exp2(s * SCALE2 - lse_ref[:1, 512 * j : 512 * j + 512])
                if masked:
                    prob = jnp.where(iota((512, 512), 0) + at <= limit, prob, 0.0)
                dv[pl.ds(at, 512), :] += matmul(prob.astype(BF16), grad)
                prob_grad = matmul_nt(v_ref[pl.ds(at, 512), :], grad)
                score = (prob * (prob_grad - delta[:1])).astype(BF16)
                dk[pl.ds(at, 512), :] += matmul(score, query)
                dq[j] += matmul_tn(score, key)
                return carry

            return body

        full = (scal[2 + 4 * j] + 1) // 512
        last = jnp.minimum(scal[2 + 4 * j + 3] + ROWS - 1, total - 1) // 512 + 1
        lax.fori_loop(0, full, step(False), 0)
        lax.fori_loop(full, last, step(True), 0)

    moves.need()
    rows8 = iota((WIDTH, SIZE), 0) % 8
    gains = w_ref[:, 384:].astype(F32)
    query_gain = jnp.sum(jnp.where(rows8 == 0, gains, 0.0), 0, keepdims=True)
    key_gain = jnp.sum(jnp.where(rows8 == 1, gains, 0.0), 0, keepdims=True)

    query_part = jnp.zeros((1, SIZE), F32)
    key_part = jnp.zeros((1, SIZE), F32)

    def head(grad, projected, gain, cos, sin):
        turned = grad * cos - swap_halves(grad) * sin
        scale = mean_scale(projected)
        normal = projected * scale
        part = jnp.sum(turned * normal, 0, keepdims=True)
        return norm_back(turned * gain, normal, scale).astype(BF16), part

    for e in range(PLACES):
        cos, sin = cos_ref[e], sin_ref[e]
        at = ROWS * (e % 4)
        query_grad = dq[e // 4, at : at + ROWS, :] * SCALE
        low[e, :, :128], part = head(query_grad, p_ref[e, :, :128], query_gain, cos, sin)
        query_part += part
        live = iota((ROWS, SIZE), 0) < scal[18 + e]
        start = scal[2 + e]
        key_grad = jnp.where(live, dk[pl.ds(start, ROWS), :], 0.0) * SCALE
        low[e, :, 128:256], part = head(key_grad, p_ref[e, :, 128:], key_gain, cos, sin)
        key_part += part
        low[e, :, 256:] = jnp.where(live, dv[pl.ds(start, ROWS), :], 0.0).astype(BF16)

        if e % 4 == 3:
            rows = low[e - 3 : e + 1].reshape(4 * ROWS, 384)
            terms = matmul_nt(rows, w_ref[:, :384]).astype(BF16)
            blocks = slice(e - 3, e + 1)
            terms_vmem[blocks] = terms.reshape(4, ROWS, WIDTH)
            for i in range(4):
                moves.push(terms_vmem.at[e - 3 + i], terms_ref.at[4 * i + e // 4])
    gains_ref[...] = jnp.where(iota((8, SIZE), 0) == 0, query_part, key_part)


def retreat(scal, head_grad, saved, weight, cos, sin, projected, after):
    outs = [((PLACES, ROWS, 384), BF16), ((8, SIZE), F32), ((PLACES, ROWS, WIDTH), BF16)]
    slots = PLACES * ROWS
    scratch = [
        pltpu.VMEM((4, 512, SIZE), F32),
        pltpu.VMEM((slots + ROWS, SIZE), F32),
        pltpu.VMEM((slots + ROWS, SIZE), F32),
        pltpu.VMEM((8, 512), F32),
        pltpu.VMEM((PLACES, ROWS, WIDTH), BF16),
    ]
    return call(
        retreat_kernel, outs, (scal, head_grad, *saved, weight, cos, sin, projected, after),
        (0,), (11,), (2,), scratch, micros=25, sends=16,
    )


def weigh_heads_kernel(moves, scal, *refs):
    tokens, (low, gains_ref, after, mine_ref, theirs_ref, grad) = refs[:8], refs[8:]
    moves.need()
    for quarter in range(4):
        part, mode = divmod(quarter, 2)
        total = jnp.zeros((256, 384), F32)
        for half in range(2):
            blocks = [places(scal, part, SEEN[mode][2 * half + i // 4], i % 4) for i in range(8)]
            rows = jnp.concatenate([low[e] for e in blocks], 0)
            total += matmul_tn(tokens[2 * quarter + half][...].reshape(8 * ROWS, 256), rows)
        grad[256 * quarter : 256 * quarter + 256, :384] = total.astype(BF16)
    rows8 = iota((WIDTH, SIZE), 0) % 8
    spot = iota((WIDTH, SIZE), 0) // 8 == iota((WIDTH, SIZE), 1)
    extra = jnp.where(rows8 == 0, gains_ref[:1], jnp.where(rows8 == 1, gains_ref[1:2], 0.0))
    grad[:, 384:] = jnp.where(spot, extra, 0.0).astype(BF16)
    for x in range(4):
        for c, ref in enumerate((mine_ref, theirs_ref)):
            block = 2 * x + (scal[37] ^ c)
            ref[x] = grad[pl.ds(pl.multiple_of(ROWS * block, ROWS), ROWS), :]


def weigh_heads(scal, tokens, low, gains, after):
    return call(
        weigh_heads_kernel, [((4, ROWS, 512), BF16)] * 2, (scal, *tokens, low, gains, after), (0,), (11,),
        scratch=[pltpu.VMEM((WIDTH, 512), BF16)], limit=20, micros=7,
    )


def feed_kernel(
    moves, scal, mixed_ref, x_ref, cot_ref, ff_ref,
    out_ref, mg_ref, send_ref, mine_ref, theirs_ref, right_ref,
    w, sems, gate, up, half, normal,
):
    core, count = scal[0], scal[1]
    copies = [pltpu.make_async_copy(ff_ref.at[u], w.at[u], sems.at[u]) for u in range(UNITS)]
    for u in (0, 1, 2, 5, 8, 3, 6, 9, 4, 7, 10):
        copies[u].start()

    def left(unit, value):
        even = jnp.concatenate([value[:, 256 * i : 256 * i + 128] for i in range(4)], 1)
        odd = jnp.concatenate([value[:, 256 * i + 128 : 256 * i + 256] for i in range(4)], 1)
        at = slice(512 * unit, 512 * unit + 512)
        mine_ref[:, at] = jnp.where(core == 0, even, odd)
        theirs_ref[:, at] = jnp.where(core == 0, odd, even)

    low_lanes = iota((ROWS, SIZE), 1) < 64
    moves.need()
    for i in range(8):
        a, b = mixed_ref[2 * i].astype(F32), mixed_ref[2 * i + 1].astype(F32)
        at = slice(128 * i, 128 * i + 128)
        half[0, :, at] = jnp.where(low_lanes, a, swap_halves(b)).astype(BF16)
        half[1, :, at] = jnp.where(low_lanes, swap_halves(a), b).astype(BF16)
    out_ref[...] = x_ref[...]
    for t in range(2):
        left(t, half[t])
        copies[t].wait()
        out_ref[...] += matmul(half[t], w[t])
    middle = out_ref[...]
    scale = mean_scale(middle)
    normal[...] = middle * scale
    normal_low = normal[...].astype(BF16)
    left(2, normal_low)
    live = iota((ROWS, 1), 0) < count
    branch = jnp.where(live, cot_ref[...], 0.0).astype(BF16)
    right_ref[:, 7 * WIDTH :] = branch
    mg_ref[...] = jnp.zeros_like(mg_ref)
    for t in range(3):
        copies[2 + t].wait()
        copies[5 + t].wait()
        copies[8 + t].wait()
        gate[...] = matmul(normal_low, w[2 + t])
        up[...] = matmul(normal_low, w[5 + t])
        g, u = gate[...], up[...]
        sig = 0.5 + 0.5 * jnp.tanh(0.5 * g)
        inner = (g * sig * u).astype(BF16)
        left(3 + t, inner)
        out_ref[...] += matmul(inner, w[8 + t])
        grad_inner = matmul_nt(branch, w[8 + t])
        gate_grad = (grad_inner * u * sig * (1.0 + g * (1.0 - sig))).astype(BF16)
        up_grad = (grad_inner * g * sig).astype(BF16)
        right_ref[:, WIDTH * (1 + t) : WIDTH * (2 + t)] = gate_grad
        right_ref[:, WIDTH * (4 + t) : WIDTH * (5 + t)] = up_grad
        mg_ref[...] += matmul_nt(gate_grad, w[2 + t])
        mg_ref[...] += matmul_nt(up_grad, w[5 + t])
    moves.flush(0, 3, 4)
    middle_grad = jnp.where(live, cot_ref[...], 0.0) + norm_back(mg_ref[...], normal[...], scale)
    mg_ref[...] = middle_grad
    attn_grad = middle_grad.astype(BF16)
    right_ref[:, :WIDTH] = attn_grad
    moves.flush(1, 5)
    first = matmul_nt(attn_grad, w[0])
    second = matmul_nt(attn_grad, w[1])
    for i in range(8):
        a, b = first[:, 128 * i : 128 * i + 128], second[:, 128 * i : 128 * i + 128]
        send_ref[2 * i] = jnp.where(low_lanes, a, swap_halves(b)).astype(BF16)
        send_ref[2 * i + 1] = jnp.where(low_lanes, swap_halves(a), b).astype(BF16)


def feed(scal, mixed, x, cotangent, ff):
    outs = [
        ((ROWS, WIDTH), F32),
        ((ROWS, WIDTH), F32),
        ((HEADS, ROWS, SIZE), BF16),
        ((ROWS, 3072), BF16),
        ((ROWS, 3072), BF16),
        ((ROWS, 8 * WIDTH), BF16),
    ]
    scratch = [
        pltpu.VMEM((UNITS, WIDTH, WIDTH), BF16),
        pltpu.SemaphoreType.DMA((UNITS,)),
        pltpu.VMEM((ROWS, WIDTH), F32),
        pltpu.VMEM((ROWS, WIDTH), F32),
        pltpu.VMEM((2, ROWS, WIDTH), BF16),
        pltpu.VMEM((ROWS, WIDTH), F32),
    ]
    return call(
        feed_kernel, outs, (scal, mixed, x, cotangent, ff), (0,), (4,), scratch=scratch,
        micros=22,
    )


def weigh_kernel(moves, scal, lm_ref, lt_ref, rm_ref, rt_ref, *refs):
    outs, (left, right), buffers = refs[:10], refs[10:12], refs[12:]
    moves.need(1, 2)
    for l in range(6):
        at = slice(512 * l, 512 * l + 512)
        left[at, :128] = lm_ref[:, at].astype(F32).T.astype(BF16)
        left[at, 128:] = lt_ref[:, at].astype(F32).T.astype(BF16)
    moves.need()
    right[:128] = rm_ref[...]
    right[128:] = rt_ref[...]
    for s, (part, mode, halves) in enumerate(SHARES):
        buffer = buffers[s]
        for n, (unit, c) in enumerate(halves):
            l, r = PAIRS[unit]
            at = WIDTH * r + COLUMNS * c
            out = matmul(left[512 * l : 512 * l + 512], right[:, at : at + COLUMNS])
            for i in range(4):
                if part == 0:
                    block = out[128 * i : 128 * i + 128]
                elif part == 1:
                    rows = [128 * x + 32 * i for x in range(4)]
                    block = jnp.concatenate([out[r : r + 32] for r in rows], 0)
                else:
                    rows = [32 * j + 8 * i for j in range(16)]
                    block = jnp.concatenate([out[r : r + 8] for r in rows], 0)
                buffer[i, n] = block.astype(BF16)
        for i, mask in enumerate(KEPT[mode]):
            moves.push(buffer.at[scal[part] ^ mask], outs[2 * s + i // 2].at[i % 2])


def weigh(scal, mine, theirs, right, right_theirs):
    outs = [((2, len(h), 128, COLUMNS), BF16) for p, m, h in SHARES for i in range(2)]
    scratch = [pltpu.VMEM((3072, 256), BF16), pltpu.VMEM((256, 8 * WIDTH), BF16)]
    scratch += [pltpu.VMEM((4, len(h), 128, COLUMNS), BF16) for p, m, h in SHARES]
    out = call(
        weigh_kernel, outs, (scal, mine, theirs, right, right_theirs), (0,), (), range(10),
        scratch, micros=9, sends=20,
    )
    return out[::2], out[1::2]


AXES = ("x", "y", "z")


def add(a, b):
    return a.astype(F32) + b.astype(F32)


def four(refs):
    return add(refs[0][...], refs[1][...]) + add(refs[2][...], refs[3][...])


def add_first_kernel(moves, *refs):
    keeps, gots, (after,), refs = refs[:5], refs[5:10], refs[10:11], refs[11:]
    new_keeps, new_sends, token = refs[:5], refs[5:10], refs[10]
    token[...] = jnp.zeros_like(token)
    for s in range(5):
        moves.need(s, 5 + s)
        new_sends[s][...] = add(keeps[s][1], gots[s][1]).astype(BF16)
        moves.flush(5 + s)
    for s in range(5):
        new_keeps[s][...] = add(keeps[s][0], gots[s][0]).astype(BF16)
        moves.flush(s)


def add_first(keeps, gots, after):
    outs = [(k.shape[1:], BF16) for k in keeps] * 2 + [((8, SIZE), F32)]
    order = [i for s in range(5) for i in (s, 5 + s)]
    out = call(
        add_first_kernel, outs, (*keeps, *gots, after), anywhere=(10,), micros=6, order=order
    )
    return out[:5], out[5:10], out[10]


COUNTS = [len(p) for p in PARTS]
SEQUENCE = (2, 3, 4, 0, 1)


def join_kernel(moves, scal, *refs):
    keeps, gots, outs, buffers = refs[:5], refs[5:10], refs[10:18], refs[18:]
    for s in SEQUENCE:
        part, mode, halves = SHARES[s]
        moves.need(1 + s, 6 + s)
        buffer, first = (buffers[1], 32 * COUNTS[1]) if part == 2 else (buffers[part], 0)
        first += 32 * len(SHARES[s - 1][2]) * mode
        for n in range(len(halves)):
            total = add(keeps[s][n], gots[s][n])
            at = first + 32 * n
            for i in range(4):
                buffer[i, at : at + 32] = total[32 * i : 32 * i + 32].astype(BF16)
        if s == 4:
            for mask in range(4):
                moves.push(buffers[1].at[scal[0] ^ mask], outs[4 + mask])
    for mask in range(4):
        moves.push(buffers[0].at[scal[1] ^ mask], outs[mask])


def join(scal, keeps, gots):
    shapes = [(32 * COUNTS[0], COLUMNS), (32 * (COUNTS[1] + COUNTS[2]), COLUMNS)]
    outs = [(shape, BF16) for shape in shapes for mask in range(4)]
    order = [1 + s for s in SEQUENCE]
    return call(
        join_kernel, outs, (scal, *keeps, *gots), (0,), (), range(8),
        [pltpu.VMEM((4, *shape), BF16) for shape in shapes], limit=20, micros=5, sends=8,
        order=order, still=range(6, 11),
    )


def add_heads_kernel(moves, scal, mine_ref, theirs_ref, *refs):
    outs, buffer = refs[:4], refs[4]
    moves.need()
    for x in range(4):
        buffer[x] = add(mine_ref[x], theirs_ref[x]).astype(BF16)
    for mask in range(4):
        moves.push(buffer.at[scal[0] ^ mask], outs[mask])


def add_heads(scal, mine, theirs):
    return call(
        add_heads_kernel, [((ROWS, 512), BF16)] * 4, (scal, mine, theirs), (0,), raw=range(4),
        scratch=[pltpu.VMEM((4, ROWS, 512), BF16)], micros=2, sends=4,
    )


def sum_heads_kernel(moves, *refs):
    moves.need()
    total = four(refs[:4])
    for f in range(HEADS):
        refs[4][f] = total[8 * f : 8 * f + 8].astype(BF16)


def sum_heads(got):
    return call(sum_heads_kernel, [((HEADS, 8, 512), BF16)], tuple(got), micros=2)[0]


def pass_on_kernel(moves, scal, *refs):
    got, outs, buffer, small = refs[:8], refs[8:16], refs[16], refs[17]
    moves.need()
    totals = [four(got[:4]), four(got[4:])]
    for part in range(3):
        total = totals[min(part, 1)]
        for n in range(COUNTS[part]):
            for i in range(4):
                at = 32 * n + 8 * i + (32 * COUNTS[1] if part == 2 else 0)
                block = total[at : at + 8].astype(BF16)
                if part < 2:
                    at = 8 * COUNTS[0] * part + 8 * n
                    buffer[i, at : at + 8] = block
                else:
                    small[i, 8 * n : 8 * n + 8] = block
        if part == 1:
            for mask in range(4):
                moves.push(buffer.at[scal[2] ^ mask], outs[mask])
    for mask in range(4):
        moves.push(small.at[scal[1] ^ mask], outs[4 + mask])


def pass_on(scal, got):
    shapes = [(8 * (COUNTS[0] + COUNTS[1]), COLUMNS), (8 * COUNTS[2], COLUMNS)]
    outs = [(shape, BF16) for shape in shapes for mask in range(4)]
    return call(
        pass_on_kernel, outs, (scal, *got), (0,), raw=range(8), limit=40, still=range(1, 9),
        scratch=[pltpu.VMEM((4, *shape), BF16) for shape in shapes], micros=4, sends=8,
    )


def finish_heads_kernel(
    moves, back_ref, q_ref, k_ref, v_ref, g1_ref, dq_ref, dk_ref, dv_ref, dg_ref, dgq_ref, dgk_ref
):
    moves.need()
    gain = column(g1_ref[...].astype(BF16).astype(F32))
    order = channel_map(True)
    dg = jnp.zeros((8, 1), F32)
    extra = jnp.zeros((8, SIZE), F32)
    for h in range(KV_HEADS):
        pair = []
        for f in (2 * h, 2 * h + 1):
            total = back_ref[f].astype(F32)
            at = slice(128 * f, 128 * f + 128)
            dq_ref[0, :, at] = total[:, :128] * gain
            w = q_ref[0, :, at].astype(BF16).astype(F32)
            dg += jnp.sum(total[:, :128] * w, 1, keepdims=True)
            extra += total[:, 384:]
            pair.append(total)
        at = slice(128 * h, 128 * h + 128)
        both = pair[0] + pair[1]
        dk = both[:, 128:256]
        dv = exact(both[:, 256:384], order)
        dk_ref[0, :, at] = dk * gain
        dv_ref[0, :, at] = dv * gain
        dg += jnp.sum(dk * k_ref[0, :, at].astype(BF16).astype(F32), 1, keepdims=True)
        dg += jnp.sum(dv * v_ref[0, :, at].astype(BF16).astype(F32), 1, keepdims=True)
    dg_ref[...] = jnp.sum(jnp.where(iota((8, 8), 0) == iota((8, 8), 1), dg, 0.0), 0, keepdims=True)
    extra = jnp.sum(extra, 1, keepdims=True)
    dgq_ref[...] = extra[0:1]
    dgk_ref[...] = extra[1:2]


def finish_heads(back, q, k, v, g1):
    outs = [((1, 8, 2048), F32)] + [((1, 8, 1024), F32)] * 2 + [((1, 8), F32)] + [((1, 1), F32)] * 2
    return call(finish_heads_kernel, outs, (back, q, k, v, g1), limit=16, micros=2)


def finish_feed_kernel(moves, *refs):
    got, more, (g_ref, u_ref, g2_ref), outs = refs[:4], refs[4:8], refs[8:11], refs[11:]
    do_ref, dg_ref, du_ref, dd_ref, gain_ref = outs
    moves.need()
    total = jnp.concatenate([four(got), four(more)], 0)
    tiles = {key: total[8 * n : 8 * n + 8] for n, key in enumerate(PIECES)}
    units = [jnp.concatenate([tiles[u, c] for c in range(4)], 1) for u in range(UNITS)]
    for t in range(2):
        do_ref[0, 8 * t : 8 * t + 8] = units[t]
    for t in range(3):
        dd_ref[0, 8 * t : 8 * t + 8] = units[8 + t]
    gain = column(g2_ref[...].astype(BF16).astype(F32))
    order = hidden_map(True)
    dg = jnp.zeros((8, 1), F32)
    for base, w_ref, out_ref in ((2, g_ref, dg_ref), (5, u_ref, du_ref)):
        tall = jnp.concatenate(
            [
                jnp.concatenate([units[base + t][:, 128 * i : 128 * i + 128] for t in range(3)], 1)
                for i in range(8)
            ],
            0,
        )
        tall = exact(tall, order)
        for i in range(8):
            at = slice(384 * i, 384 * i + 384)
            grad = tall[8 * i : 8 * i + 8]
            dg += jnp.sum(grad * w_ref[0, :, at].astype(BF16).astype(F32), 1, keepdims=True)
            out_ref[0, :, at] = grad * gain
    gain_ref[...] = jnp.sum(jnp.where(iota((8, 8), 0) == iota((8, 8), 1), dg, 0.0), 0, keepdims=True)


def finish_feed(got, gate, up, g2):
    outs = [
        ((1, 16, 1024), F32), ((1, 8, 3072), F32), ((1, 8, 3072), F32), ((1, 24, 1024), F32), ((1, 8), F32),
    ]
    return call(
        finish_feed_kernel, outs, (*got, gate, up, g2), limit=16, micros=3, still=range(8)
    )


def finish_input_kernel(moves, part_ref, x_ref, mg_ref, out_ref):
    moves.need()
    x = x_ref[...]
    scale = mean_scale(x)
    out_ref[...] = mg_ref[...] + norm_back(part_ref[...].astype(F32), x * scale, scale)


def finish_input(part, x, middle_grad):
    return call(
        finish_input_kernel, [((ROWS, WIDTH), F32)], (part, x, middle_grad), limit=16, micros=2
    )[0]


def other(v):
    return lax.ppermute(v, "core", [(0, 1), (1, 0)])


def trade(v, axes):
    return lax.all_to_all(v, axes, split_axis=0, concat_axis=0, tiled=True)


def exchange(v, axis, mask):
    return lax.ppermute(v, axis, [(i, i ^ mask) for i in range(4)])


def swap(terms, axis):
    return [terms[0]] + [exchange(terms[mask], axis, mask) for mask in (1, 3, 2)]


def in_order(v):
    return [v[0], v[1], v[3], v[2]]


def shards(
    block_input, counts, query_weight, key_matrix, value_matrix, out_weight, gate_weight,
    up_weight, down_weight, attn_gain, mlp_gain, query_gain, key_gain, cotangent,
):
    place = lax.axis_index(TOKENS)
    group = lax.axis_index(("x", "core"))
    core = lax.axis_index("core")
    own = lax.axis_index(ALL).reshape(1).astype(jnp.int32)
    ff_pack = pack_feed(out_weight, gate_weight, up_weight, down_weight, mlp_gain)
    ff = lax.all_gather(ff_pack, ALL, axis=1, tiled=True)
    early, late = prepare(block_input, ff_pack)
    blocks = [swap([early] * 4, "y"), swap([late] * 4, "z")]
    head_send = pack_heads(
        own, query_gain, key_gain, query_weight, key_matrix, value_matrix, attn_gain, ff_pack
    )
    head_weights = jnp.stack(in_order(swap([trade(head_send, TOKENS).reshape(ROWS, 512)] * 4, "x")))
    head_weights = (head_weights, other(head_weights))
    tokens = []
    for block, axis in zip(blocks, "zy"):
        block = jnp.stack(in_order(block))
        for mode in range(2):
            piece = block[:, :, 256 * mode : 256 * mode + 256]
            both = jnp.stack([piece, exchange(piece, axis, MASKS[mode][0])])
            tokens += [both, exchange(both, axis, MASKS[mode][1])]

    group_counts = lax.dynamic_index_in_dim(counts, group, 0, keepdims=False)
    starts = jnp.cumsum(group_counts) - group_counts
    own_count = lax.dynamic_index_in_dim(group_counts, place, 0, keepdims=False)
    scal = jnp.concatenate(
        [place.reshape(1), jnp.sum(group_counts).reshape(1), starts, group_counts]
        + [lax.axis_index(a).reshape(1) for a in ("y", "z", "x", "core")]
    ).astype(jnp.int32)
    inverse = ROPE_BASE ** (-(jnp.arange(64, dtype=F32) * 2.0 / SIZE))
    position = starts[:, None] + jnp.arange(ROWS, dtype=jnp.int32)[None, :]
    angles = position.astype(F32)[:, :, None] * inverse
    cosine, sine = jnp.cos(angles), jnp.sin(angles)
    cos = jnp.concatenate([cosine, cosine], -1)
    sin = jnp.concatenate([-sine, sine], -1)

    mixed_head, *saved, projected, head_weight = attend(scal, tokens, head_weights, cos, sin)
    mixed = trade(mixed_head, TOKENS)
    block_output, middle_grad, grad_send, mine, theirs, right = feed(
        jnp.stack([core, own_count]).astype(jnp.int32), mixed, block_input, cotangent, ff
    )
    head_grad = trade(grad_send, TOKENS)

    chip = jnp.stack([lax.axis_index(a) for a in AXES]).astype(jnp.int32)
    keeps, sends = weigh(chip, mine, other(theirs), right, other(right))
    sends, head_grad = lax.optimization_barrier((sends, head_grad))

    def step(sends, order):
        return [
            exchange(v, FIRST[part], MASKS[mode][order])
            for v, (part, mode, halves) in zip(sends, SHARES)
        ]

    gots = step(sends, 0)
    low, head_gains, token_terms = retreat(
        scal, head_grad, [mixed_head] + saved, head_weight, cos, sin, projected, sends[0]
    )
    gots, token_terms = lax.optimization_barrier((gots, token_terms))
    token_sum = lax.psum_scatter(
        token_terms.reshape(PLACES * ROWS, WIDTH), ("z", "y"), scatter_dimension=0, tiled=True
    )
    keeps, sends, token = add_first(keeps, gots, head_gains)
    gots = step(sends, 1)
    head_mine, head_theirs = weigh_heads(scal, tokens, low, head_gains, token)
    heads = add_heads(chip, head_mine, other(head_theirs))
    terms = join(chip, keeps, gots)
    got = swap(terms[:4], "y") + swap(terms[4:], "x")
    heads, early = lax.optimization_barrier((heads, got[5]))
    head_back = trade(sum_heads(swap(heads, "x")), TOKENS)
    terms = pass_on(chip, got)
    got = swap(terms[:4], "z") + swap(terms[4:], "y")
    query_grad, key_grad, value_grad, attn_gain_grad, query_gain_grad, key_gain_grad = finish_heads(
        head_back, query_weight, key_matrix, value_matrix, attn_gain
    )
    input_grad = finish_input(token_sum, block_input, middle_grad)
    got, others = lax.optimization_barrier((got, (input_grad, query_gain_grad)))
    out_grad, gate_grad, up_grad, down_grad, mlp_gain_grad = finish_feed(
        got, gate_weight, up_weight, mlp_gain
    )
    return (
        block_output,
        input_grad,
        query_grad,
        key_grad,
        value_grad,
        out_grad,
        gate_grad,
        up_grad,
        down_grad,
        attn_gain_grad,
        mlp_gain_grad,
        query_gain_grad,
        key_gain_grad,
    )


def solution(mesh):
    fine = Mesh(mesh.devices.reshape(4, 2, 4, 4), ALL)
    tokens = P(ALL, None)
    weight = P(None, ALL, None)
    gain = P(None, ALL)
    return jax.shard_map(
        shards,
        mesh=fine,
        in_specs=(tokens, P()) + (weight,) * 7 + (gain,) * 4 + (tokens,),
        out_specs=(tokens, tokens) + (weight,) * 7 + (gain,) * 4,
        check_vma=False,
    )
```
